32 devices in a mesh: section: 2 (over core), shard: 4 (over z), rep: 4 (over y, x).
Axes of the slice: x: 2, y: 2, z: 4, core: 2. Of those that a mesh axis runs over, the one named last changes fastest.
Arguments:
- tokens: bfloat16 [3072, 1024], P(('shard', 'rep')), may hold values from -6 to 6
- doc_lengths: int32 [32, 4], P(('shard', 'rep')), may hold values from 1 to 48, 96 in all within a row
- heads_weight: bfloat16 [2, 1024, 3072], P('section', 'shard'), may hold values from -0.1875 to 0.1875
- merge_weight: bfloat16 [2, 1024, 1024], P('section', 'shard'), may hold values from -0.75 to 0.75
- up_weight: bfloat16 [2, 1024, 4096], P('section', 'shard'), may hold values from -0.1875 to 0.1875
- down_weight: bfloat16 [2, 4096, 1024], P('section', 'shard'), may hold values from -0.125 to 0.125
- first_gain: bfloat16 [2, 1024], P('section', 'shard'), may hold values from 0.5 to 1.5
- first_shift: bfloat16 [2, 1024], P('section', 'shard'), may hold values from -3 to 3
- query_bias: bfloat16 [2, 1024], P('section', 'shard'), may hold values from -3 to 3
- value_bias: bfloat16 [2, 1024], P('section', 'shard'), may hold values from -3 to 3
- output_bias: bfloat16 [2, 1024], P('section', 'shard'), may hold values from -3 to 3
- second_gain: bfloat16 [2, 1024], P('section', 'shard'), may hold values from 0.5 to 1.5
- second_shift: bfloat16 [2, 1024], P('section', 'shard'), may hold values from -3 to 3
- up_bias: bfloat16 [2, 4096], P('section', 'shard'), may hold values from -3 to 3
- down_bias: bfloat16 [2, 1024], P('section', 'shard'), may hold values from -3 to 3
- cotangent: bfloat16 [3072, 1024], P(('shard', 'rep')), may hold values from -6 to 6
Outputs:
- activations: bfloat16 [2, 3072, 1024], P('section', ('shard', 'rep'))
- input_grads: bfloat16 [2, 3072, 1024], P('section', ('shard', 'rep'))
- grad_heads_weight: float32 [2, 1024, 3072], P('section', 'shard')
- grad_merge_weight: float32 [2, 1024, 1024], P('section', 'shard')
- grad_up_weight: float32 [2, 1024, 4096], P('section', 'shard')
- grad_down_weight: float32 [2, 4096, 1024], P('section', 'shard')
- grad_first_gain: float32 [2, 1024], P('section', 'shard')
- grad_first_shift: float32 [2, 1024], P('section', 'shard')
- grad_query_bias: float32 [2, 1024], P('section', 'shard')
- grad_value_bias: float32 [2, 1024], P('section', 'shard')
- grad_output_bias: float32 [2, 1024], P('section', 'shard')
- grad_second_gain: float32 [2, 1024], P('section', 'shard')
- grad_second_shift: float32 [2, 1024], P('section', 'shard')
- grad_up_bias: float32 [2, 4096], P('section', 'shard')
- grad_down_bias: float32 [2, 1024], P('section', 'shard')
The draws below stay inside these ranges and needn't reach their ends.
Inputs may be any that keep to these rules, and one draw needn't show every extreme that they name: `doc_lengths`: each row holds, in order, the lengths of the 4 sequences packed into one slot of 96 rows; they sum to 96.
All inputs are finite; a program needn't handle non-finite values.
Results may differ from the reference program's by a relative error of at most 0.02.
Values may be sent and summed in bfloat16 or wider, within the bound.
No kernel may reach another device: no remote copies, remote signals or barrier semaphores. Data moves between devices by JAX's collectives and lax.ppermute only.
A program may use at most 192 MiB of HBM per device.

```python
import math
import jax
import jax.numpy as jnp
import numpy as np
from jax import lax

D = 1024
HEADS = 16
FF = 4096
ROWS = 96
DOCS = 4
SLOTS = 32
TOKENS = 3072
N_SECTION = 2


def block_levels(own_key, extent, cuts, smallest, high):
    gain = 1.0
    for dim, blocks in cuts:
        steps = jax.random.uniform(jax.random.fold_in(jax.random.fold_in(own_key, 6), dim), (blocks,), jnp.float32, smallest / len(cuts), high / len(cuts))
        gain = gain * jnp.repeat(jnp.exp(steps), extent[dim] // blocks).reshape((-1,) + (1,) * (len(extent) - 1 - dim))
    return gain


def length_profile(amount, total, limit, slope):
    weights = [(1 << 20) // math.isqrt(grade ** slope) + 1 for grade in range(2, amount + 1)]
    surplus, holding = total - limit - (amount - 1), [1] * (amount - 1)
    while surplus > 0:
        free = [i for i in range(amount - 1) if holding[i] < limit]
        mass, budget = sum([weights[i] for i in free]), surplus
        for i in free:
            addition = min(limit - holding[i], max(1, budget * weights[i] // mass), surplus)
            holding[i] = holding[i] + addition
            surplus = surplus - addition
    return np.array([limit] + holding)


def ragged_sizes(stream_key, count, total, bound, lean):
    if count == 2:
        one = jax.random.randint(stream_key, (), max(1, total - bound), min(bound, total - 1) + 1)
        return jnp.stack([one, total - one])
    sizes = jnp.asarray(length_profile(count, total, bound, lean), jnp.int32)
    twos = (count - 1) // 2
    giver, sink = sizes[1:1 + 2 * twos:2], sizes[2:2 + 2 * twos:2]
    room = jnp.minimum(giver - 1, bound - sink)
    passed = jax.random.randint(jax.random.fold_in(stream_key, 1), (twos,), 0, 1 << 20) % (room + 1)
    sizes = sizes.at[1:1 + 2 * twos:2].set(giver - passed).at[2:2 + 2 * twos:2].set(sink + passed)
    return sizes[jax.random.permutation(jax.random.fold_in(stream_key, 2), count)]


def scatter_about(rng, shape, scale, most, split=(), kind=jnp.bfloat16):
    array = scale * jax.random.normal(rng, shape, jnp.float32)
    if split:
        array = array * block_levels(rng, shape, split, -0.22, 0.18)
    return jnp.clip(array, -most, most).astype(kind)


def setup_inputs(seed: int = 0) -> dict:
    seeds = jax.random.split(jax.random.key(seed), 17)
    tokens = scatter_about(seeds[0], (TOKENS, D), 1.0, 6.0, ((0, 16),))
    doc_lengths = jax.vmap(lambda own: ragged_sizes(own, DOCS, ROWS, ROWS // 2, 2))(jax.random.split(seeds[1], SLOTS)).reshape((SLOTS, DOCS)).astype(jnp.int32)
    heads_weight = scatter_about(seeds[2], (N_SECTION, D, 3 * D), D ** -0.5, 0.1875, ((0, 2), (1, 4)))
    merge_weight = scatter_about(seeds[3], (N_SECTION, D, D), (D // 16) ** -0.5, 0.75, ((0, 2), (1, 4)))
    up_weight = scatter_about(seeds[4], (N_SECTION, D, FF), D ** -0.5, 0.1875, ((0, 2), (1, 4)))
    down_weight = scatter_about(seeds[5], (N_SECTION, FF, D), (FF // 2) ** -0.5, 0.125, ((0, 2), (1, 4)))
    first_gain = jnp.clip(1.0 + 0.1 * jax.random.normal(seeds[6], (N_SECTION, D), jnp.float32), 0.5, 1.5).astype(jnp.bfloat16)
    first_shift = scatter_about(seeds[7], (N_SECTION, D), 0.3, 3.0, ((0, 2), (1, 4)))
    query_bias = scatter_about(seeds[8], (N_SECTION, D), 0.3, 3.0, ((0, 2), (1, 4)))
    value_bias = scatter_about(seeds[9], (N_SECTION, D), 0.3, 3.0, ((0, 2), (1, 4)))
    output_bias = scatter_about(seeds[10], (N_SECTION, D), 0.3, 3.0, ((0, 2), (1, 4)))
    second_gain = jnp.clip(1.0 + 0.1 * jax.random.normal(seeds[11], (N_SECTION, D), jnp.float32), 0.5, 1.5).astype(jnp.bfloat16)
    second_shift = scatter_about(seeds[12], (N_SECTION, D), 0.3, 3.0, ((0, 2), (1, 4)))
    up_bias = scatter_about(seeds[13], (N_SECTION, FF), 0.3, 3.0, ((0, 2), (1, 4)))
    down_bias = scatter_about(seeds[14], (N_SECTION, D), 0.3, 3.0, ((0, 2), (1, 4)))
    cotangent = scatter_about(seeds[15], (TOKENS, D), 1.0, 6.0, ((0, 16),))
    return dict(tokens=tokens, doc_lengths=doc_lengths, heads_weight=heads_weight, merge_weight=merge_weight, up_weight=up_weight, down_weight=down_weight, first_gain=first_gain, first_shift=first_shift, query_bias=query_bias, value_bias=value_bias, output_bias=output_bias, second_gain=second_gain, second_shift=second_shift, up_bias=up_bias, down_bias=down_bias, cotangent=cotangent)


@jax.custom_vjp
def low(v):
    return lax.optimization_barrier(v.astype(jnp.bfloat16)).astype(jnp.float32)

@jax.custom_vjp
def low_back(v):
    return v

def low_keep(v):
    return (low(v), None)

def low_pass(kept, grad):
    return (grad,)

def back_keep(v):
    return (v, None)

def back_low(kept, grad):
    return (low(grad),)
low.defvjp(low_keep, low_pass)
low_back.defvjp(back_keep, back_low)
NORM_EPS = 1e-05
GELU_COEF = 0.7978845608028654

def gelu_tanh(entries):
    return 0.5 * entries * (1.0 + jnp.tanh(GELU_COEF * (entries + 0.044715 * entries * entries * entries)))

def norm_rows(entries, norm_gain, norm_shift):
    centre = lax.optimization_barrier(jnp.mean(entries, axis=-1, keepdims=True))
    centred = entries - centre
    spread = lax.optimization_barrier(jnp.mean(centred * centred, axis=-1, keepdims=True))
    return centred * lax.rsqrt(spread + NORM_EPS) * norm_gain + norm_shift

def visible_mask(lengths, row_count):
    doc_ends = jnp.cumsum(lengths)
    position = jnp.arange(row_count, dtype=jnp.int32)
    segment = lax.optimization_barrier(jnp.sum((position[:, None] >= doc_ends[None, :]).astype(jnp.int32), axis=1))
    causal = position[None, :] <= position[:, None]
    return jnp.logical_and(segment[:, None] == segment[None, :], causal)

def highest(left, right):
    return jnp.dot(left, right, precision=lax.Precision.HIGHEST)

def attend(slot_args):
    joint_rows, lengths = slot_args
    row_count = joint_rows.shape[0]
    head_size = D // HEADS
    score_scale = 1.0 / math.sqrt(head_size)
    query_heads = joint_rows[:, :D].reshape(row_count, HEADS, head_size)
    key_heads = joint_rows[:, D:2 * D].reshape(row_count, HEADS, head_size)
    value_heads = joint_rows[:, 2 * D:].reshape(row_count, HEADS, head_size)
    scores = jnp.einsum('qhd,khd->hqk', query_heads, key_heads, precision=lax.Precision.HIGHEST) * score_scale
    scores = low_back(scores)
    visible = visible_mask(lengths, row_count)
    scores = jnp.where(visible[None], scores, -1e+30)
    row_top = lax.optimization_barrier(jnp.max(scores, axis=-1, keepdims=True))
    log_total = row_top + jnp.log(lax.optimization_barrier(jnp.sum(jnp.exp(scores - row_top), axis=-1, keepdims=True)))
    softmax_low = low(jnp.exp(scores - log_total))
    attended = jnp.einsum('hqk,khd->qhd', softmax_low, value_heads, precision=lax.Precision.HIGHEST)
    return attended.reshape(row_count, D)

def residual_block(hidden, weights, doc_lengths):
    heads_weight, merge_weight, up_weight, down_weight, first_gain, first_shift, query_bias, value_bias, output_bias, second_gain, second_shift, up_bias, down_bias = weights
    normed = low(norm_rows(hidden, first_gain, first_shift))
    joint_bias = jnp.concatenate([query_bias, jnp.zeros_like(query_bias), value_bias])
    joint_rows = low_back(low(highest(normed, heads_weight) + joint_bias))
    slot_rows = joint_rows.reshape(SLOTS, ROWS, 3 * D)
    attended = lax.map(jax.checkpoint(attend), (slot_rows, doc_lengths)).reshape(SLOTS * ROWS, D)
    attended = low_back(low(attended))
    middle = hidden + low_back(highest(attended, merge_weight) + output_bias)
    second = low(norm_rows(middle, second_gain, second_shift))
    before = low_back(highest(second, up_weight) + up_bias)
    active = low(gelu_tanh(before))
    return middle + low_back(highest(active, down_weight) + down_bias)

def reference(tokens, doc_lengths, heads_weight, merge_weight, up_weight, down_weight, first_gain, first_shift, query_bias, value_bias, output_bias, second_gain, second_shift, up_bias, down_bias, cotangent):
    weights = tuple((matrix.astype(jnp.float32) for matrix in (heads_weight, merge_weight, up_weight, down_weight, first_gain, first_shift, query_bias, value_bias, output_bias, second_gain, second_shift, up_bias, down_bias)))
    start_rows = tokens.astype(jnp.float32)
    offsets = jnp.zeros((N_SECTION - 1, start_rows.shape[0], D), jnp.float32)

    def forward(start_rows, weights, offsets):
        hidden = start_rows
        layer_outputs = []
        result = hidden
        for section_number in range(N_SECTION):
            result = residual_block(hidden, tuple((matrix[section_number] for matrix in weights)), doc_lengths)
            layer_outputs.append(result)
            if section_number + 1 < N_SECTION:
                hidden = low_back(low(result)) + offsets[section_number]
        return (result, jnp.stack(layer_outputs))
    result, pullback, layer_outputs = jax.vjp(forward, start_rows, weights, offsets, has_aux=True)
    grad_start, grad_weights, grad_offsets = pullback(cotangent.astype(jnp.float32))
    activations = layer_outputs.astype(jnp.bfloat16)
    input_grads = jnp.concatenate([grad_start[None], grad_offsets], axis=0).astype(jnp.bfloat16)
    return (activations, input_grads, grad_weights[0], grad_weights[1], grad_weights[2], grad_weights[3], grad_weights[4], grad_weights[5], grad_weights[6], grad_weights[7], grad_weights[8], grad_weights[9], grad_weights[10], grad_weights[11], grad_weights[12])
```

```python
import math

import jax
import jax.numpy as jnp
from jax import lax
from jax.experimental import pallas as pl
from jax.experimental.pallas import tpu as pltpu
from jax.sharding import PartitionSpec as P

HEADS = 16
NORM_EPS = 1e-05
GELU_COEF = 0.7978845608028654
GELU_CUBE = 0.044715
LOW = jnp.bfloat16
F32 = jnp.float32


def dot(left, right):
    return jnp.dot(left, right, preferred_element_type=F32)


def dot_t(left, right):
    return lax.dot_general(left, right, (((1,), (1,)), ((), ())), preferred_element_type=F32)


def t_dot(left, right):
    return lax.dot_general(left, right, (((0,), (0,)), ((), ())), preferred_element_type=F32)


def call(kernel, outs, args, flops=0):
    nbytes = sum(a.size * a.dtype.itemsize for a in args) + sum(
        math.prod(o.shape) * jnp.dtype(o.dtype).itemsize for o in outs
    )
    vmem = pl.BlockSpec(memory_space=pltpu.VMEM)
    return pl.pallas_call(
        kernel,
        out_shape=outs,
        in_specs=[vmem] * len(args),
        out_specs=[vmem] * len(outs),
        compiler_params=pltpu.CompilerParams(vmem_limit_bytes=50 * 2**20),
        cost_estimate=pl.CostEstimate(flops=flops, bytes_accessed=nbytes, transcendentals=0),
    )(*args)


def sds(shape, dtype=LOW):
    return jax.ShapeDtypeStruct(shape, dtype)


def normalized(rows):
    centred = rows - jnp.mean(rows, axis=-1, keepdims=True)
    spread = jnp.mean(centred * centred, axis=-1, keepdims=True)
    rstd = lax.rsqrt(spread + NORM_EPS)
    return centred * rstd, rstd


def affine(xhat, gain_ref, shift_ref):
    return (xhat * gain_ref[...].astype(F32) + shift_ref[...].astype(F32)).astype(LOW)


def column_sum(rows):
    return jnp.sum(rows, axis=0, keepdims=True)


def joined(refs):
    return jnp.concatenate([ref[...] for ref in refs], axis=0)


def added(refs):
    total = refs[0][...].astype(F32)
    for ref in refs[1:]:
        total = total + ref[...].astype(F32)
    return total


def store_blocks(refs, rows):
    size = refs[0].shape[0]
    for number, ref in enumerate(refs):
        ref[...] = rows[number * size : (number + 1) * size].astype(ref.dtype)


def norm_kernel(rows_ref, gain_ref, shift_ref, out_ref):
    xhat, _ = normalized(rows_ref[...].astype(F32))
    out_ref[...] = affine(xhat, gain_ref, shift_ref)


def head_masks(width, head_size):
    lane = lax.broadcasted_iota(jnp.int32, (1, width), 1)
    return [
        jnp.logical_and(lane >= h * head_size, lane < (h + 1) * head_size).astype(F32)
        for h in range(width // head_size)
    ]


def stacked_heads(rows, masks):
    wide = rows.astype(F32)
    return jnp.concatenate([(wide * m).astype(LOW) for m in masks], axis=0)


def folded_heads(stacked, masks):
    size = stacked.shape[0] // len(masks)
    total = stacked[:size] * masks[0]
    for h in range(1, len(masks)):
        total = total + stacked[h * size : (h + 1) * size] * masks[h]
    return total


def make_attention_forward(parts, head_size):
    scale = 1.0 / math.sqrt(head_size)

    def kernel(*refs):
        x_refs, (wh, jb, vis, wm) = refs[:parts], refs[parts : parts + 4]
        x_all, joint, probs, attended = refs[parts + 4 : parts + 8]
        blocks = refs[parts + 8 :]
        rows = joined(x_refs)
        x_all[...] = rows
        joint[...] = (dot(rows, wh[...]) + jb[...].astype(F32)).astype(LOW)
        width = wm.shape[0]
        masks = head_masks(width, head_size)
        slots, size, _ = vis.shape
        for b in range(slots):
            at = slice(b * size, (b + 1) * size)
            query = stacked_heads(joint[at, :width], masks)
            scores = dot_t(query, joint[at, width : 2 * width]) * scale
            seen = jnp.concatenate([vis[b]] * len(masks), axis=0) > 0.0
            scores = jnp.where(seen, scores, -1e30)
            top = jnp.max(scores, axis=-1, keepdims=True)
            weights = jnp.exp(scores - top)
            share = weights * (1.0 / jnp.sum(weights, axis=-1, keepdims=True))
            probs[b] = share
            mixed = dot(share.astype(LOW), joint[at, 2 * width :])
            attended[at, :] = folded_heads(mixed, masks).astype(LOW)
        store_blocks(blocks, dot(attended[...], wm[...]))

    return kernel


def make_attention_backward(parts, head_size):
    scale = 1.0 / math.sqrt(head_size)

    def kernel(*refs):
        g_refs, (wm, wh, joint, probs) = refs[:parts], refs[parts : parts + 4]
        g_all, g_joint, g_query, g_value = refs[parts + 4 : parts + 8]
        blocks = refs[parts + 8 :]
        rows = joined(g_refs)
        g_all[...] = rows
        g_attended = dot_t(rows, wm[...]).astype(LOW)
        width = wm.shape[0]
        masks = head_masks(width, head_size)
        slots, _, size = probs.shape
        for b in range(slots):
            at = slice(b * size, (b + 1) * size)
            query = stacked_heads(joint[at, :width], masks)
            g_heads = stacked_heads(g_attended[at], masks)
            share = probs[b]
            g_probs = dot_t(g_heads, joint[at, 2 * width :])
            inner = jnp.sum(share * g_probs, axis=-1, keepdims=True)
            g_scores = (share * (g_probs - inner)).astype(LOW)
            g_q = folded_heads(dot(g_scores, joint[at, width : 2 * width]), masks) * scale
            g_joint[at, :width] = g_q.astype(LOW)
            g_joint[at, width : 2 * width] = (t_dot(g_scores, query) * scale).astype(LOW)
            g_joint[at, 2 * width :] = t_dot(share.astype(LOW), g_heads).astype(LOW)
        store_blocks(blocks, dot_t(g_joint[...], wh[...]))
        g_query[...] = column_sum(g_joint[:, :width].astype(F32))
        g_value[...] = column_sum(g_joint[:, 2 * width :].astype(F32))

    return kernel


def make_middle(parts):
    def kernel(hidden, *refs):
        terms, (bias, gain, shift) = refs[:parts], refs[parts : parts + 3]
        middle, second = refs[parts + 3 :]
        rows = hidden[...].astype(F32) + added(terms) + bias[...].astype(F32)
        middle[...] = rows
        xhat, _ = normalized(rows)
        second[...] = affine(xhat, gain, shift)

    return kernel


def make_block_end(parts, with_norm):
    def kernel(middle, *refs):
        terms, bias = refs[:parts], refs[parts]
        rest = refs[parts + 1 :]
        rows = (middle[...] + added(terms) + bias[...].astype(F32)).astype(LOW)
        if with_norm:
            gain, shift, out, normed = rest
            xhat, _ = normalized(rows.astype(F32))
            normed[...] = affine(xhat, gain, shift)
        else:
            (out,) = rest
        out[...] = rows

    return kernel


def make_mlp_forward(parts):
    def kernel(*refs):
        x_refs, (wu, ub, wd) = refs[:parts], refs[parts : parts + 3]
        x_all, before, active = refs[parts + 3 : parts + 6]
        blocks = refs[parts + 6 :]
        rows = joined(x_refs)
        x_all[...] = rows
        value = dot(rows, wu[...]) + ub[...].astype(F32)
        before[...] = value
        inner = jnp.tanh(GELU_COEF * (value + GELU_CUBE * value * value * value))
        active[...] = (0.5 * value * (1.0 + inner)).astype(LOW)
        if blocks:
            store_blocks(blocks, dot(active[...], wd[...]))

    return kernel


def make_mlp_backward(parts):
    def kernel(*refs):
        g_refs, (wd, wu, before) = refs[:parts], refs[parts : parts + 3]
        g_all, g_before, g_bias = refs[parts + 3 : parts + 6]
        blocks = refs[parts + 6 :]
        rows = joined(g_refs)
        g_all[...] = rows
        g_active = dot_t(rows, wd[...])
        value = before[...]
        inner = jnp.tanh(GELU_COEF * (value + GELU_CUBE * value * value * value))
        slope = 0.5 * (1.0 + inner) + 0.5 * value * (1.0 - inner * inner) * GELU_COEF * (
            1.0 + 3.0 * GELU_CUBE * value * value
        )
        result = (g_active * slope).astype(LOW)
        g_before[...] = result
        g_bias[...] = column_sum(result.astype(F32))
        store_blocks(blocks, dot_t(result, wu[...]))

    return kernel


def norm_back(grad, xhat, rstd, gain_ref):
    e = grad * gain_ref[...].astype(F32)
    mean_e = jnp.mean(e, axis=-1, keepdims=True)
    mean_ex = jnp.mean(e * xhat, axis=-1, keepdims=True)
    return rstd * (e - mean_e - xhat * mean_ex)


def make_middle_backward(parts):
    def kernel(grad_out, middle, *refs):
        terms, gain = refs[:parts], refs[parts]
        g_middle, g_merge, g_gain, g_shift, g_output, g_down = refs[parts + 1 :]
        grad = added(terms)
        xhat, rstd = normalized(middle[...])
        own = grad_out[...].astype(F32)
        rows = own + norm_back(grad, xhat, rstd, gain)
        g_middle[...] = rows
        low_rows = rows.astype(LOW)
        g_merge[...] = low_rows
        g_gain[...] = column_sum(grad * xhat)
        g_shift[...] = column_sum(grad)
        g_output[...] = column_sum(low_rows.astype(F32))
        g_down[...] = column_sum(own)

    return kernel


def make_first_backward(parts):
    def kernel(g_middle, hidden, *refs):
        terms, gain = refs[:parts], refs[parts]
        g_hidden, g_gain, g_shift = refs[parts + 1 :]
        grad = added(terms)
        xhat, rstd = normalized(hidden[...].astype(F32))
        g_hidden[...] = (g_middle[...] + norm_back(grad, xhat, rstd, gain)).astype(LOW)
        g_gain[...] = column_sum(grad * xhat)
        g_shift[...] = column_sum(grad)

    return kernel


def pick_columns_kernel(matrix, left, right, out):
    block = left.shape[0]
    step = left.shape[1]
    for m in range(out.shape[1] // step):
        first = dot(matrix[:, 2 * m * block : (2 * m + 1) * block], left[...])
        second = dot(matrix[:, (2 * m + 1) * block : (2 * m + 2) * block], right[...])
        out[:, m * step : (m + 1) * step] = (first + second).astype(LOW)


def make_spread_columns(parts):
    def kernel(*refs):
        pieces, place, out = refs[:parts], refs[parts], refs[parts + 1]
        size = place.shape[1]
        wide = place.shape[2]
        for m in range(out.shape[1] // wide):
            total = dot(pieces[0][:, m * size : (m + 1) * size], place[0])
            for k in range(1, parts):
                total = total + dot(pieces[k][:, m * size : (m + 1) * size], place[k])
            out[:, m * wide : (m + 1) * wide] = total

    return kernel


def swap(block):
    return lax.ppermute(block, "section", [(0, 1), (1, 0)])


def from_peers(blocks, axis, section=None):
    count = lax.axis_size(axis)
    received = []
    for k in range(1, count):
        if section is None:
            pairs = [(i, i ^ k) for i in range(count)]
            received.append(lax.ppermute(blocks[k], axis, pairs))
        else:
            pairs = [(section * count + i, section * count + (i ^ k)) for i in range(count)]
            received.append(lax.ppermute(blocks[k], ("section", axis), pairs))
    return [blocks[0]] + received


def gathered_blocks(block, axis, section=None):
    return from_peers([block] * lax.axis_size(axis), axis, section)


def body(
    tokens,
    doc_lengths,
    heads_weight,
    merge_weight,
    up_weight,
    down_weight,
    first_gain,
    first_shift,
    query_bias,
    value_bias,
    output_bias,
    second_gain,
    second_shift,
    up_bias,
    down_bias,
    cotangent,
):
    sections = lax.axis_size("section")
    shards = lax.axis_size("shard")
    reps = lax.axis_size("rep")
    assert sections == 2
    core = lax.axis_index("section")
    shard = lax.axis_index("shard")
    rep = lax.axis_index("rep")
    on_first = core == 0

    features = tokens.shape[1]
    slot_rows = tokens.shape[0] // doc_lengths.shape[0]
    slots = doc_lengths.shape[0] // sections
    n = slots * slot_rows
    all_rows = reps * n
    head_size = features // HEADS
    width = features // reps
    ff = up_weight.shape[2]
    ff_own = ff // reps
    depth = features // shards
    strided = HEADS % (shards * reps) == 0
    head_run = (HEADS // (shards * reps)) * head_size if strided else width

    def rows_of_core(array, which):
        return lax.dynamic_index_in_dim(
            array.reshape((sections, array.shape[0] // sections) + array.shape[1:]),
            which,
            0,
            keepdims=False,
        )

    vectors = (
        first_gain,
        first_shift,
        query_bias,
        value_bias,
        output_bias,
        second_gain,
        second_shift,
        down_bias,
        up_bias,
    )
    packed = jnp.concatenate([v.reshape(-1, depth) for v in vectors], axis=0)
    vector_rows = packed.shape[0]
    shard_order = gathered_blocks(packed, "shard")

    def in_order(pieces, index):
        count = len(pieces)
        result = []
        for j in range(count):
            total = pieces[0]
            for k in range(1, count):
                total = jnp.where(index == (j ^ k), pieces[k], total)
            result.append(total)
        return jnp.stack(result)

    own_vectors = in_order(shard_order, shard)
    other_vectors = swap(own_vectors)
    section_vectors = (
        jnp.where(on_first, own_vectors, other_vectors),
        jnp.where(on_first, other_vectors, own_vectors),
    )

    def vector(s, number):
        return section_vectors[s][:, number, :].reshape(1, features)

    def own_heads_part(flat):
        if strided:
            cut = flat.reshape(shards, reps, head_run)
            return lax.dynamic_index_in_dim(cut, rep, 1, keepdims=False).reshape(1, width)
        return lax.dynamic_index_in_dim(flat.reshape(reps, width), rep, 0, keepdims=False).reshape(
            1, width
        )

    def up_vector(s):
        flat = section_vectors[s][:, 8:, :].reshape(shards, reps, ff_own // shards)
        return lax.dynamic_index_in_dim(flat, rep, 1, keepdims=False).reshape(1, ff_own)

    def joint_vector(s):
        query = own_heads_part(vector(s, 2))
        value = own_heads_part(vector(s, 3))
        return jnp.concatenate([query, jnp.zeros_like(query), value], axis=1)

    if strided:
        lane = jnp.arange(reps * head_run, dtype=jnp.int32)[:, None]
        place = jnp.arange(2 * head_run, dtype=jnp.int32)[None, :]
        hit = lane == rep * head_run + place % head_run
        left = jnp.logical_and(hit, place < head_run).astype(LOW)
        right = jnp.logical_and(hit, place >= head_run).astype(LOW)
        heads_part = call(
            pick_columns_kernel, [sds((depth, 3 * width))], [heads_weight[0], left, right]
        )[0]
        merge_part = lax.dynamic_slice_in_dim(merge_weight[0], rep * head_run, head_run, 0)
    else:
        heads_part = lax.dynamic_index_in_dim(
            heads_weight.reshape(depth, 3, reps, width), rep, 2, keepdims=False
        ).reshape(depth, 3 * width)
        merge_part = merge_weight[0]
    up_part = lax.dynamic_index_in_dim(
        up_weight.reshape(depth, shards, reps, ff_own // shards), rep, 2, keepdims=False
    ).reshape(depth, ff_own)
    down_part = lax.dynamic_slice_in_dim(
        down_weight[0], rep * (ff_own // shards), ff_own // shards, 0
    )

    weights = []
    halves = []
    for part in (heads_part, merge_part, up_part, down_part):
        kept = rows_of_core(part, core)
        other = swap(rows_of_core(part, 1 - core))
        halves.append((jnp.where(on_first, kept, other), jnp.where(on_first, other, kept)))
    for s in range(sections):
        full = [
            lax.all_gather(pair[s], ("shard", "section"), axis=0, tiled=True) for pair in halves
        ]
        if not strided:
            full[1] = lax.dynamic_slice_in_dim(full[1], rep * width, width, 0)
        weights.append(full)

    own_lengths = rows_of_core(doc_lengths, core)
    lengths = jnp.concatenate(gathered_blocks(own_lengths, "rep"), axis=0)
    ends = jnp.cumsum(lengths, axis=1)
    position = jnp.arange(slot_rows, dtype=jnp.int32)
    segment = jnp.sum((position[None, :, None] >= ends[:, None, :]).astype(jnp.int32), axis=2)
    visible = jnp.logical_and(
        segment[:, :, None] == segment[:, None, :], position[None, None, :] <= position[None, :, None]
    ).astype(F32)
    slot_count = reps * slots

    own_tokens = rows_of_core(tokens, core)
    own_cotangent = rows_of_core(cotangent, core)
    block_shapes = [sds((n, features))] * reps
    attention_flops = 2 * all_rows * features * 4 * width
    mlp_flops = 4 * all_rows * features * ff_own

    hidden = own_tokens
    normed = call(
        norm_kernel, [sds((n, features))], [hidden, vector(0, 0), vector(0, 1)]
    )[0]
    saved = []
    outputs = []
    for s in range(sections):
        wh, wm, wu, wd = weights[s]
        results = call(
            make_attention_forward(reps, head_size),
            [
                sds((all_rows, features)),
                sds((all_rows, 3 * width)),
                sds((slot_count, (width // head_size) * slot_rows, slot_rows), F32),
                sds((all_rows, width)),
            ]
            + block_shapes,
            gathered_blocks(normed, "rep") + [wh, joint_vector(s), visible, wm],
            attention_flops,
        )
        normed_all, joint, probs, attended = results[:4]
        terms = from_peers(results[4:], "rep")
        middle, second = call(
            make_middle(reps),
            [sds((n, features), F32), sds((n, features))],
            [hidden] + terms + [vector(s, 4), vector(s, 5), vector(s, 6)],
        )
        results = call(
            make_mlp_forward(reps),
            [sds((all_rows, features)), sds((all_rows, ff_own), F32), sds((all_rows, ff_own))]
            + block_shapes,
            gathered_blocks(second, "rep") + [wu, up_vector(s), wd],
            mlp_flops,
        )
        second_all, before, active = results[:3]
        terms = from_peers(results[3:], "rep")
        saved.append((hidden, normed_all, joint, probs, attended, middle, second_all, before, active))
        if s + 1 < sections:
            hidden, normed = call(
                make_block_end(reps, True),
                [sds((n, features)), sds((n, features))],
                [middle] + terms + [vector(s, 7), vector(s + 1, 0), vector(s + 1, 1)],
            )
            outputs.append(hidden)
        else:
            outputs.append(
                call(
                    make_block_end(reps, False),
                    [sds((n, features))],
                    [middle] + terms + [vector(s, 7)],
                )[0]
            )

    grad_out = own_cotangent
    hidden_grads = [None] * sections
    vector_grads = [None] * sections
    weight_grads = [None] * sections

    def over_slots(left, right):
        product = t_dot(left, right).astype(LOW)
        return lax.psum_scatter(product, ("shard", "section"), scatter_dimension=0, tiled=True)

    for s in reversed(range(sections)):
        wh, wm, wu, wd = weights[s]
        hidden, normed_all, joint, probs, attended, middle, second_all, before, active = saved[s]
        row = sds((1, features), F32)
        results = call(
            make_mlp_backward(reps),
            [sds((all_rows, features)), sds((all_rows, ff_own)), sds((1, ff_own), F32)]
            + block_shapes,
            gathered_blocks(grad_out, "rep") + [wd, wu, before],
            mlp_flops,
        )
        down_all, before_all, up_sum = results[:3]
        terms = from_peers(results[3:], "rep")
        grad_down = over_slots(active, down_all)
        grad_up = over_slots(second_all, before_all)
        g_middle, g_merge, second_gain_sum, second_shift_sum, output_sum, down_sum = call(
            make_middle_backward(reps),
            [sds((n, features), F32), sds((n, features))] + [row] * 4,
            [grad_out, middle] + terms + [vector(s, 5)],
        )
        results = call(
            make_attention_backward(reps, head_size),
            [
                sds((all_rows, features)),
                sds((all_rows, 3 * width)),
                sds((1, width), F32),
                sds((1, width), F32),
            ]
            + block_shapes,
            gathered_blocks(g_merge, "rep") + [wm, wh, joint, probs],
            2 * attention_flops,
        )
        merge_all, joint_all, query_sum, value_sum = results[:4]
        terms = from_peers(results[4:], "rep")
        grad_heads = over_slots(normed_all, joint_all)
        if strided:
            grad_merge = over_slots(attended, merge_all)
        else:
            product = t_dot(attended, merge_all).astype(LOW)
            spread = lax.dynamic_update_slice_in_dim(
                jnp.zeros((features, features), LOW), product, rep * width, 0
            )
            grad_merge = lax.psum_scatter(
                spread, ("shard", "section"), scatter_dimension=0, tiled=True
            )
        grad_out, first_gain_sum, first_shift_sum = call(
            make_first_backward(reps),
            [sds((n, features)), row, row],
            [g_middle, hidden] + terms + [vector(s, 0)],
        )
        hidden_grads[s] = grad_out

        def placed_heads(part):
            if strided:
                wide = jnp.zeros((shards, reps, head_run), F32)
                part = part.reshape(shards, 1, head_run)
                return lax.dynamic_update_slice_in_dim(wide, part, rep, 1).reshape(shards, 1, depth)
            wide = jnp.zeros((reps, width), F32)
            return lax.dynamic_update_slice_in_dim(wide, part, rep, 0).reshape(shards, 1, depth)

        wide_up = lax.dynamic_update_slice_in_dim(
            jnp.zeros((shards, reps, ff_own // shards), F32),
            up_sum.reshape(shards, 1, ff_own // shards),
            rep,
            1,
        ).reshape(shards, -1, depth)
        vector_grads[s] = jnp.concatenate(
            [
                first_gain_sum.reshape(shards, 1, depth),
                first_shift_sum.reshape(shards, 1, depth),
                placed_heads(query_sum),
                placed_heads(value_sum),
                output_sum.reshape(shards, 1, depth),
                second_gain_sum.reshape(shards, 1, depth),
                second_shift_sum.reshape(shards, 1, depth),
                down_sum.reshape(shards, 1, depth),
                wide_up,
            ],
            axis=1,
        )
        weight_grads[s] = (grad_heads, grad_merge, grad_up, grad_down)

    own_sum = jnp.where(on_first, vector_grads[0], vector_grads[1])
    other_sum = jnp.where(on_first, vector_grads[1], vector_grads[0])
    own_sum = own_sum + swap(other_sum)
    pieces = from_peers(
        [
            lax.dynamic_index_in_dim(own_sum, shard ^ k, 0, keepdims=False)
            for k in range(shards)
        ],
        "shard",
    )
    total = sum(pieces[1:], pieces[0])
    pieces = gathered_blocks(total, "rep")
    total = sum(pieces[1:], pieces[0])
    singles = [total[number].reshape(1, depth) for number in range(8)]
    grad_up_bias = total[8:].reshape(1, -1)

    def owned(number):
        parts = []
        for s in range(sections):
            mine = weight_grads[s][number]
            theirs = lax.ppermute(mine, "section", [(1 - s, s)])
            parts.append(jnp.concatenate([mine, theirs] if s == 0 else [theirs, mine], axis=0))
        return parts

    def over_reps(number):
        parts = owned(number)
        lists = [gathered_blocks(parts[s], "rep", s) for s in range(sections)]
        return [jnp.where(on_first, a, b) for a, b in zip(*lists)]

    heads_pieces = over_reps(0)
    if strided:
        lane = jnp.arange(head_run, dtype=jnp.int32)[:, None]
        place = jnp.arange(reps * head_run, dtype=jnp.int32)[None, :]
        places = jnp.stack(
            [(place == (rep ^ k) * head_run + lane).astype(LOW) for k in range(reps)]
        )
        grad_heads = call(
            make_spread_columns(reps),
            [sds((depth, 3 * features), F32)],
            heads_pieces + [places],
        )[0][None]
        merge_pieces = over_reps(1)
        grad_merge = jnp.zeros((reps, head_run, features), F32)
        for k, piece in enumerate(merge_pieces):
            grad_merge = lax.dynamic_update_slice_in_dim(
                grad_merge, piece.astype(F32)[None], rep ^ k, 0
            )
        grad_merge = grad_merge.reshape(1, depth, features)
    else:
        grad_heads = jnp.zeros((depth, 3, reps, width), F32)
        for k, piece in enumerate(heads_pieces):
            grad_heads = lax.dynamic_update_slice_in_dim(
                grad_heads, piece.astype(F32).reshape(depth, 3, 1, width), rep ^ k, 2
            )
        grad_heads = grad_heads.reshape(1, depth, 3 * features)
        parts = owned(1)
        grad_merge = lax.psum(jnp.where(on_first, parts[0], parts[1]), "rep").astype(F32)[None]

    grad_up = jnp.zeros((depth, shards, reps, ff_own // shards), F32)
    for k, piece in enumerate(over_reps(2)):
        grad_up = lax.dynamic_update_slice_in_dim(
            grad_up, piece.astype(F32).reshape(depth, shards, 1, ff_own // shards), rep ^ k, 2
        )
    grad_up = grad_up.reshape(1, depth, ff)
    grad_down = jnp.zeros((reps, ff_own // shards, features), F32)
    for k, piece in enumerate(over_reps(3)):
        grad_down = lax.dynamic_update_slice_in_dim(
            grad_down, piece.astype(F32)[None], rep ^ k, 0
        )
    grad_down = grad_down.reshape(1, ff // shards, features)

    def by_section(pair):
        own = jnp.where(on_first, pair[0], pair[1])
        other = swap(jnp.where(on_first, pair[1], pair[0]))
        return jnp.concatenate(
            [jnp.where(on_first, own, other), jnp.where(on_first, other, own)], axis=0
        )[None]

    activations = by_section(outputs)
    input_grads = by_section(hidden_grads)
    (
        grad_first_gain,
        grad_first_shift,
        grad_query,
        grad_value,
        grad_output,
        grad_second_gain,
        grad_second_shift,
        grad_down_bias,
    ) = singles
    return (
        activations,
        input_grads,
        grad_heads,
        grad_merge,
        grad_up,
        grad_down,
        grad_first_gain,
        grad_first_shift,
        grad_query,
        grad_value,
        grad_output,
        grad_second_gain,
        grad_second_shift,
        grad_up_bias,
        grad_down_bias,
    )


def solution(mesh):
    rows = P(("shard", "rep"), None)
    matrix = P("section", "shard", None)
    line = P("section", "shard")
    return jax.shard_map(
        body,
        mesh=mesh,
        in_specs=(rows, rows) + (matrix,) * 4 + (line,) * 9 + (rows,),
        out_specs=(P("section", ("shard", "rep"), None),) * 2 + (matrix,) * 4 + (line,) * 9,
        check_vma=False,
    )
```

```python
import math

import jax
import jax.numpy as jnp
from jax import lax
from jax.experimental import pallas as pl
from jax.experimental.pallas import tpu as pltpu
from jax.sharding import PartitionSpec as P

HEADS = 16
TIE_DOWN = 3
TIE_UP = 4
COPY_DOWN = 5
NORM_EPS = 1e-05
GELU_COEF = 0.7978845608028654
GELU_CUBE = 0.044715
LOW = jnp.bfloat16
F32 = jnp.float32


def dot(left, right):
    return jnp.dot(left, right, preferred_element_type=F32)


def dot_t(left, right):
    return lax.dot_general(left, right, (((1,), (1,)), ((), ())), preferred_element_type=F32)


def t_dot(left, right):
    return lax.dot_general(left, right, (((0,), (0,)), ((), ())), preferred_element_type=F32)


def call(kernel, outs, args, flops=0, scalars=None):
    nbytes = sum(a.size * a.dtype.itemsize for a in args) + sum(
        math.prod(o.shape) * jnp.dtype(o.dtype).itemsize for o in outs
    )
    vmem = pl.BlockSpec(memory_space=pltpu.VMEM)
    return pl.pallas_call(
        kernel,
        out_shape=outs,
        in_specs=[pl.BlockSpec(memory_space=pltpu.SMEM)] * (scalars is not None)
        + [vmem] * len(args),
        out_specs=[vmem] * len(outs),
        compiler_params=pltpu.CompilerParams(vmem_limit_bytes=40 * 2**20),
        cost_estimate=pl.CostEstimate(flops=flops, bytes_accessed=nbytes, transcendentals=0),
    )(*(([] if scalars is None else [scalars]) + list(args)))


def sds(shape, dtype=LOW):
    return jax.ShapeDtypeStruct(shape, dtype)


def normalized(rows):
    centred = rows - jnp.mean(rows, axis=-1, keepdims=True)
    spread = jnp.mean(centred * centred, axis=-1, keepdims=True)
    rstd = lax.rsqrt(spread + NORM_EPS)
    return centred * rstd, rstd


def affine(xhat, gain_ref, shift_ref):
    return (xhat * gain_ref[...].astype(F32) + shift_ref[...].astype(F32)).astype(LOW)


def column_sum(rows):
    return jnp.sum(rows, axis=0, keepdims=True)


def joined(refs):
    return jnp.concatenate([ref[...] for ref in refs], axis=0)


def added(refs):
    total = refs[0][...].astype(F32)
    for ref in refs[1:]:
        total = total + ref[...].astype(F32)
    return total


def store_blocks(refs, rows):
    size = refs[0].shape[0]
    for number, ref in enumerate(refs):
        ref[...] = rows[number * size : (number + 1) * size].astype(ref.dtype)


def norm_kernel(rows_ref, gain_ref, shift_ref, out_ref):
    xhat, _ = normalized(rows_ref[...].astype(F32))
    out_ref[...] = affine(xhat, gain_ref, shift_ref)


def head_masks(width, head_size):
    lane = lax.broadcasted_iota(jnp.int32, (1, width), 1)
    return [
        jnp.logical_and(lane >= h * head_size, lane < (h + 1) * head_size).astype(F32)
        for h in range(width // head_size)
    ]


def stacked_heads(rows, masks):
    wide = rows.astype(F32)
    return jnp.concatenate([(wide * m).astype(LOW) for m in masks], axis=0)


def folded_heads(stacked, masks):
    size = stacked.shape[0] // len(masks)
    total = stacked[:size] * masks[0]
    for h in range(1, len(masks)):
        total = total + stacked[h * size : (h + 1) * size] * masks[h]
    return total


def make_attention_forward(parts, head_size):
    scale = 1.0 / math.sqrt(head_size)

    def kernel(*refs):
        x_refs, (wh, jb, vis, wm) = refs[:parts], refs[parts : parts + 4]
        x_all, joint, probs, attended = refs[parts + 4 : parts + 8]
        blocks = refs[parts + 8 :]
        rows = joined(x_refs)
        x_all[...] = rows
        joint[...] = (dot(rows, wh[...]) + jb[...].astype(F32)).astype(LOW)
        width = wm.shape[0]
        masks = head_masks(width, head_size)
        slots, size, _ = vis.shape
        for b in range(slots):
            at = slice(b * size, (b + 1) * size)
            query = stacked_heads(joint[at, :width], masks)
            scores = dot_t(query, joint[at, width : 2 * width]) * scale
            seen = jnp.concatenate([vis[b]] * len(masks), axis=0) > 0.0
            scores = jnp.where(seen, scores, -1e30)
            top = jnp.max(scores, axis=-1, keepdims=True)
            weights = jnp.exp(scores - top)
            share = weights * (1.0 / jnp.sum(weights, axis=-1, keepdims=True))
            probs[b] = share
            mixed = dot(share.astype(LOW), joint[at, 2 * width :])
            attended[at, :] = folded_heads(mixed, masks).astype(LOW)
        store_blocks(blocks, dot(attended[...], wm[...]))

    return kernel


def make_attention_backward(parts, head_size):
    scale = 1.0 / math.sqrt(head_size)

    def kernel(*refs):
        g_refs, (wm, wh, joint, probs) = refs[:parts], refs[parts : parts + 4]
        g_all, g_joint, g_query, g_value = refs[parts + 4 : parts + 8]
        blocks = refs[parts + 8 :]
        rows = joined(g_refs)
        g_all[...] = rows
        g_attended = dot_t(rows, wm[...]).astype(LOW)
        width = wm.shape[0]
        masks = head_masks(width, head_size)
        slots, _, size = probs.shape
        for b in range(slots):
            at = slice(b * size, (b + 1) * size)
            query = stacked_heads(joint[at, :width], masks)
            g_heads = stacked_heads(g_attended[at], masks)
            share = probs[b]
            g_probs = dot_t(g_heads, joint[at, 2 * width :])
            inner = jnp.sum(share * g_probs, axis=-1, keepdims=True)
            g_scores = (share * (g_probs - inner)).astype(LOW)
            g_q = folded_heads(dot(g_scores, joint[at, width : 2 * width]), masks) * scale
            g_joint[at, :width] = g_q.astype(LOW)
            g_joint[at, width : 2 * width] = (t_dot(g_scores, query) * scale).astype(LOW)
            g_joint[at, 2 * width :] = t_dot(share.astype(LOW), g_heads).astype(LOW)
        store_blocks(blocks, dot_t(g_joint[...], wh[...]))
        g_query[...] = column_sum(g_joint[:, :width].astype(F32))
        g_value[...] = column_sum(g_joint[:, 2 * width :].astype(F32))

    return kernel


def make_middle(parts):
    def kernel(hidden, *refs):
        terms, (bias, gain, shift) = refs[:parts], refs[parts : parts + 3]
        middle, second = refs[parts + 3 :]
        rows = hidden[...].astype(F32) + added(terms) + bias[...].astype(F32)
        middle[...] = rows
        xhat, _ = normalized(rows)
        second[...] = affine(xhat, gain, shift)

    return kernel


def make_block_end(parts, with_norm):
    def kernel(middle, *refs):
        terms, bias = refs[:parts], refs[parts]
        rest = refs[parts + 1 :]
        rows = (middle[...] + added(terms) + bias[...].astype(F32)).astype(LOW)
        if with_norm:
            gain, shift, out, normed = rest
            xhat, _ = normalized(rows.astype(F32))
            normed[...] = affine(xhat, gain, shift)
        else:
            (out,) = rest
        out[...] = rows

    return kernel


def make_mlp_forward(parts):
    def kernel(*refs):
        x_refs, (wu, ub, wd) = refs[:parts], refs[parts : parts + 3]
        x_all, before, active = refs[parts + 3 : parts + 6]
        blocks = refs[parts + 6 :]
        rows = joined(x_refs)
        x_all[...] = rows
        value = dot(rows, wu[...]) + ub[...].astype(F32)
        before[...] = value
        inner = jnp.tanh(GELU_COEF * (value + GELU_CUBE * value * value * value))
        active[...] = (0.5 * value * (1.0 + inner)).astype(LOW)
        if blocks:
            store_blocks(blocks, dot(active[...], wd[...]))

    return kernel


def make_mlp_backward(parts):
    def kernel(*refs):
        g_refs, (wd, wu, before) = refs[:parts], refs[parts : parts + 3]
        g_all, g_before, g_bias = refs[parts + 3 : parts + 6]
        blocks = refs[parts + 6 :]
        rows = joined(g_refs)
        g_all[...] = rows
        g_active = dot_t(rows, wd[...])
        value = before[...]
        inner = jnp.tanh(GELU_COEF * (value + GELU_CUBE * value * value * value))
        slope = 0.5 * (1.0 + inner) + 0.5 * value * (1.0 - inner * inner) * GELU_COEF * (
            1.0 + 3.0 * GELU_CUBE * value * value
        )
        result = (g_active * slope).astype(LOW)
        g_before[...] = result
        g_bias[...] = column_sum(result.astype(F32))
        store_blocks(blocks, dot_t(result, wu[...]))

    return kernel


def norm_back(grad, xhat, rstd, gain_ref):
    e = grad * gain_ref[...].astype(F32)
    mean_e = jnp.mean(e, axis=-1, keepdims=True)
    mean_ex = jnp.mean(e * xhat, axis=-1, keepdims=True)
    return rstd * (e - mean_e - xhat * mean_ex)


def make_middle_backward(parts):
    def kernel(grad_out, middle, *refs):
        terms, gain = refs[:parts], refs[parts]
        g_middle, g_merge, g_gain, g_shift, g_output, g_down = refs[parts + 1 :]
        grad = added(terms)
        xhat, rstd = normalized(middle[...])
        own = grad_out[...].astype(F32)
        rows = own + norm_back(grad, xhat, rstd, gain)
        g_middle[...] = rows
        low_rows = rows.astype(LOW)
        g_merge[...] = low_rows
        g_gain[...] = column_sum(grad * xhat)
        g_shift[...] = column_sum(grad)
        g_output[...] = column_sum(low_rows.astype(F32))
        g_down[...] = column_sum(own)

    return kernel


def make_first_backward(parts):
    def kernel(g_middle, hidden, *refs):
        terms, gain = refs[:parts], refs[parts]
        g_hidden, g_gain, g_shift = refs[parts + 1 :]
        grad = added(terms)
        xhat, rstd = normalized(hidden[...].astype(F32))
        g_hidden[...] = (g_middle[...] + norm_back(grad, xhat, rstd, gain)).astype(LOW)
        g_gain[...] = column_sum(grad * xhat)
        g_shift[...] = column_sum(grad)

    return kernel


def pick_columns_kernel(matrix, left, right, out):
    block = left.shape[0]
    step = left.shape[1]
    for m in range(out.shape[1] // step):
        first = dot(matrix[:, 2 * m * block : (2 * m + 1) * block], left[...])
        second = dot(matrix[:, (2 * m + 1) * block : (2 * m + 2) * block], right[...])
        out[:, m * step : (m + 1) * step] = (first + second).astype(LOW)


def make_spread_columns(parts):
    def kernel(*refs):
        pieces, place, out = refs[:parts], refs[parts], refs[parts + 1]
        size = place.shape[1]
        wide = place.shape[2]
        for m in range(out.shape[1] // wide):
            total = dot(pieces[0][:, m * size : (m + 1) * size], place[0])
            for k in range(1, parts):
                total = total + dot(pieces[k][:, m * size : (m + 1) * size], place[k])
            out[:, m * wide : (m + 1) * wide] = total

    return kernel


def at_block(index, size):
    return pl.ds(pl.multiple_of(index * size, size), size)


def prepare_attention_kernel(where, heads, merge, left, right, kept, sent):
    core, rep = where[0], where[1]
    block, step = left.shape
    run = step // 2
    half = kept.shape[0]
    width = kept.shape[1] // 4
    packed = []
    for m in range(3 * width // step):
        first = dot(heads[:, 2 * m * block : (2 * m + 1) * block], left[...])
        second = dot(heads[:, (2 * m + 1) * block : (2 * m + 2) * block], right[...])
        packed.append((first + second).astype(LOW))
    own = merge[at_block(rep, run), :]
    packed.append(
        jnp.concatenate(
            [own[:, j * width : (j + 1) * width] for j in range(2 * half // run)], axis=0
        )
    )
    rows = jnp.concatenate(packed, axis=1)
    first = core == 0
    kept[...] = jnp.where(first, rows[:half], rows[half:])
    sent[...] = jnp.where(first, rows[half:], rows[:half])


def prepare_mlp_kernel(where, up, down, kept, sent):
    core, rep = where[0], where[1]
    half = kept.shape[0] // 2
    ff_own = kept.shape[1]
    run = 2 * half
    reps = up.shape[1] // ff_own
    for target, which in ((kept, core), (sent, 1 - core)):
        rows = at_block(which, half)
        for m in range(ff_own // run):
            target[:half, m * run : (m + 1) * run] = up[rows, at_block(m * reps + rep, run)]
        target[half:, :] = down[at_block(2 * rep + which, half), :]


def make_assemble_attention(shards):
    def kernel(where, *refs):
        core, shard = where[0], where[2]
        heads, merge = refs[2 * shards :]
        half = refs[0].shape[0]
        width = merge.shape[0]
        run = width // shards
        for number, ref in enumerate(refs[: 2 * shards]):
            source = lax.rem(shard - number % shards + shards, shards)
            which = core if number < shards else 1 - core
            heads[at_block(2 * source + which, half), :] = ref[:, : 3 * width]
            for j in range(half // run):
                merge[at_block(source, run), at_block(which * (half // run) + j, width)] = ref[
                    j * run : (j + 1) * run, 3 * width :
                ]

    return kernel


def make_assemble_mlp(shards):
    def kernel(where, *refs):
        core, shard = where[0], where[2]
        up, down = refs[2 * shards :]
        half = refs[0].shape[0] // 2
        for number, ref in enumerate(refs[: 2 * shards]):
            source = lax.rem(shard - number % shards + shards, shards)
            which = core if number < shards else 1 - core
            rows = at_block(2 * source + which, half)
            up[rows, :] = ref[:half, :]
            down[rows, :] = ref[half:, :]

    return kernel


def split_by_core(core, product, kept, sent, shards):
    half = product.shape[0] // (2 * shards)
    first = core == 0
    for b in range(shards):
        one = product[2 * b * half : (2 * b + 1) * half]
        two = product[(2 * b + 1) * half : (2 * b + 2) * half]
        kept[b * half : (b + 1) * half, : one.shape[1]] = jnp.where(first, one, two)
        sent[b * half : (b + 1) * half, : one.shape[1]] = jnp.where(first, two, one)


def make_weight_gradient(shards):
    def kernel(where, left, right, kept, sent):
        split_by_core(where[0], t_dot(left[...], right[...]).astype(LOW), kept, sent, shards)

    return kernel


def make_attention_gradient(shards):
    def kernel(where, normed, joint, attended, merge, kept, sent):
        core = where[0]
        split_by_core(core, t_dot(normed[...], joint[...]).astype(LOW), kept, sent, shards)
        product = t_dot(attended[...], merge[...]).astype(LOW)
        width = product.shape[0]
        run = width // shards
        half = kept.shape[0] // shards
        count = half // run
        first = core == 0
        for b in range(shards):
            rows = product[b * run : (b + 1) * run]
            for j in range(count):
                one = rows[:, j * width : (j + 1) * width]
                two = rows[:, (count + j) * width : (count + j + 1) * width]
                at = slice(b * half + j * run, b * half + (j + 1) * run)
                kept[at, 3 * width :] = jnp.where(first, one, two)
                sent[at, 3 * width :] = jnp.where(first, two, one)

    return kernel


def chosen(core, refs, number, count):
    return jnp.where(core == 0, refs[number][...], refs[count + number][...])


def make_place_attention(parts):
    def kernel(where, *refs):
        core, rep = where[0], where[1]
        place, heads, merge = refs[2 * parts :]
        run = place.shape[1]
        wide = place.shape[2]
        width = heads.shape[1] // (3 * parts)
        pieces = [chosen(core, refs, k, parts) for k in range(parts)]
        for m in range(heads.shape[1] // wide):
            total = dot(pieces[0][:, m * run : (m + 1) * run], place[0])
            for k in range(1, parts):
                total = total + dot(pieces[k][:, m * run : (m + 1) * run], place[k])
            heads[:, m * wide : (m + 1) * wide] = total
        for k in range(parts):
            for j in range(pieces[k].shape[0] // run):
                merge[at_block(jnp.bitwise_xor(rep, k), run), j * width : (j + 1) * width] = pieces[
                    k
                ][j * run : (j + 1) * run, 3 * width :].astype(F32)

    return kernel


def make_place_up(parts):
    def kernel(where, *refs):
        core, rep = where[0], where[1]
        out = refs[2 * parts]
        run = out.shape[0]
        for k in range(parts):
            piece = chosen(core, refs, k, parts).astype(F32)
            for m in range(piece.shape[1] // run):
                out[:, at_block(m * parts + jnp.bitwise_xor(rep, k), run)] = piece[
                    :, m * run : (m + 1) * run
                ]

    return kernel


def make_place_down(parts):
    def kernel(where, *refs):
        core, rep = where[0], where[1]
        out = refs[2 * parts]
        for k in range(parts):
            piece = chosen(core, refs, k, parts).astype(F32)
            out[at_block(jnp.bitwise_xor(rep, k), piece.shape[0]), :] = piece

    return kernel


def swap(block):
    return lax.ppermute(block, "section", [(0, 1), (1, 0)])


def from_peers(blocks, axis, section=None):
    count = lax.axis_size(axis)
    received = []
    for k in range(1, count):
        if section is None:
            pairs = [(i, i ^ k) for i in range(count)]
            received.append(lax.ppermute(blocks[k], axis, pairs))
        else:
            pairs = [(section * count + i, section * count + (i ^ k)) for i in range(count)]
            received.append(lax.ppermute(blocks[k], ("section", axis), pairs))
    return [blocks[0]] + received


def after(value, other):
    return lax.optimization_barrier((value, other))[0]


def ring_gather(block):
    count = lax.axis_size("shard")
    blocks = [block]
    for _ in range(count - 1):
        blocks.append(
            lax.ppermute(blocks[-1], "shard", [(i, (i + 1) % count) for i in range(count)])
        )
    return blocks + [swap(b) for b in blocks]


class GradientSum:
    def __init__(self, pair, section, tie=None, copy=None):
        self.section, self.tie, self.copy, self.age = section, tie, copy, 0
        self.state, self.stage = list(pair), 0

    def advance(self):
        self.age += 1
        if self.age in (1, self.tie, self.copy):
            self.next_stage()
            return True
        return False

    def next_stage(self):
        self.stage += 1
        s = self.section
        if self.stage == 1:
            kept, arrived = self.state[0], swap(self.state[1])
            self.state = (kept.astype(F32) + arrived.astype(F32)).astype(LOW)
        elif self.stage == 2:
            self.state = lax.psum_scatter(self.state, "shard", scatter_dimension=0, tiled=True)
        elif self.stage == 3:
            theirs = lax.ppermute(self.state, "section", [(1 - s, s)])
            order = [self.state, theirs] if s == 0 else [theirs, self.state]
            self.state = gathered_blocks(jnp.concatenate(order, axis=0), "rep", s)

    def finish(self):
        while self.stage < 3:
            self.next_stage()
        return self.state


def window(waiting, tasks, new=()):
    tied = [task for task in tasks if task.advance()] + list(new)
    tasks.extend(new)
    waiting, states = lax.optimization_barrier((waiting, [task.state for task in tied]))
    for task, state in zip(tied, states):
        task.state = state
    return waiting


def gathered_blocks(block, axis, section=None):
    return from_peers([block] * lax.axis_size(axis), axis, section)


def body(
    tokens,
    doc_lengths,
    heads_weight,
    merge_weight,
    up_weight,
    down_weight,
    first_gain,
    first_shift,
    query_bias,
    value_bias,
    output_bias,
    second_gain,
    second_shift,
    up_bias,
    down_bias,
    cotangent,
):
    sections = lax.axis_size("section")
    shards = lax.axis_size("shard")
    reps = lax.axis_size("rep")
    assert sections == 2
    core = lax.axis_index("section")
    shard = lax.axis_index("shard")
    rep = lax.axis_index("rep")
    on_first = core == 0

    features = tokens.shape[1]
    slot_rows = tokens.shape[0] // doc_lengths.shape[0]
    slots = doc_lengths.shape[0] // sections
    n = slots * slot_rows
    all_rows = reps * n
    head_size = features // HEADS
    width = features // reps
    ff = up_weight.shape[2]
    ff_own = ff // reps
    depth = features // shards
    strided = HEADS % (shards * reps) == 0
    head_run = (HEADS // (shards * reps)) * head_size if strided else width
    fast = strided and depth == reps * head_run and (ff_own // shards) == depth
    fast = fast and ff_own == features and depth % 256 == 0 and width == depth
    where = jnp.stack([core, rep, shard]).astype(jnp.int32)

    def rows_of_core(array, which):
        return lax.dynamic_index_in_dim(
            array.reshape((sections, array.shape[0] // sections) + array.shape[1:]),
            which,
            0,
            keepdims=False,
        )

    vectors = (
        first_gain,
        first_shift,
        query_bias,
        value_bias,
        output_bias,
        second_gain,
        second_shift,
        down_bias,
        up_bias,
    )
    packed = jnp.concatenate([v.reshape(-1, depth) for v in vectors], axis=0)
    vector_rows = packed.shape[0]
    shard_order = gathered_blocks(packed, "shard")

    def in_order(pieces, index):
        count = len(pieces)
        result = []
        for j in range(count):
            total = pieces[0]
            for k in range(1, count):
                total = jnp.where(index == (j ^ k), pieces[k], total)
            result.append(total)
        return jnp.stack(result)

    own_vectors = in_order(shard_order, shard)
    other_vectors = swap(own_vectors)
    section_vectors = (
        jnp.where(on_first, own_vectors, other_vectors),
        jnp.where(on_first, other_vectors, own_vectors),
    )

    def vector(s, number):
        return section_vectors[s][:, number, :].reshape(1, features)

    def own_heads_part(flat):
        if strided:
            cut = flat.reshape(shards, reps, head_run)
            return lax.dynamic_index_in_dim(cut, rep, 1, keepdims=False).reshape(1, width)
        return lax.dynamic_index_in_dim(flat.reshape(reps, width), rep, 0, keepdims=False).reshape(
            1, width
        )

    def up_vector(s):
        flat = section_vectors[s][:, 8:, :].reshape(shards, reps, ff_own // shards)
        return lax.dynamic_index_in_dim(flat, rep, 1, keepdims=False).reshape(1, ff_own)

    def joint_vector(s):
        query = own_heads_part(vector(s, 2))
        value = own_heads_part(vector(s, 3))
        return jnp.concatenate([query, jnp.zeros_like(query), value], axis=1)

    weights = []
    if fast:
        lane = jnp.arange(reps * head_run, dtype=jnp.int32)[:, None]
        column = jnp.arange(2 * head_run, dtype=jnp.int32)[None, :]
        hit = lane == rep * head_run + column % head_run
        left = jnp.logical_and(hit, column < head_run).astype(LOW)
        right = jnp.logical_and(hit, column >= head_run).astype(LOW)
        half = sds((depth // 2, 4 * width))
        kept_a, sent_a = call(
            prepare_attention_kernel,
            [half, half],
            [heads_weight[0], merge_weight[0], left, right],
            scalars=where,
        )
        whole = sds((depth, ff_own))
        other_a = swap(sent_a)
        kept_b, sent_b = call(
            prepare_mlp_kernel,
            [whole, whole],
            [up_weight[0], down_weight[0]],
            scalars=after(where, other_a),
        )
        other_b = swap(sent_b)

    def attention_weights(s, then):
        mine = on_first if s == 0 else jnp.logical_not(on_first)
        blocks = ring_gather(after(jnp.where(mine, kept_a, other_a), then))
        outs = [sds((features, 3 * width)), sds((width, features))]
        return call(make_assemble_attention(shards), outs, blocks, scalars=where), blocks

    def mlp_weights(s, then):
        mine = on_first if s == 0 else jnp.logical_not(on_first)
        blocks = ring_gather(after(jnp.where(mine, kept_b, other_b), then))
        outs = [sds((features, ff_own)), sds((ff_own, features))]
        return call(make_assemble_mlp(shards), outs, blocks, scalars=where), blocks

    if fast:
        first_pair, blocks_a = attention_weights(0, other_a)
        weights.append(list(first_pair))
    else:
        if strided:
            lane = jnp.arange(reps * head_run, dtype=jnp.int32)[:, None]
            place = jnp.arange(2 * head_run, dtype=jnp.int32)[None, :]
            hit = lane == rep * head_run + place % head_run
            left = jnp.logical_and(hit, place < head_run).astype(LOW)
            right = jnp.logical_and(hit, place >= head_run).astype(LOW)
            heads_part = call(
                pick_columns_kernel, [sds((depth, 3 * width))], [heads_weight[0], left, right]
            )[0]
            merge_part = lax.dynamic_slice_in_dim(merge_weight[0], rep * head_run, head_run, 0)
        else:
            heads_part = lax.dynamic_index_in_dim(
                heads_weight.reshape(depth, 3, reps, width), rep, 2, keepdims=False
            ).reshape(depth, 3 * width)
            merge_part = merge_weight[0]
        up_part = lax.dynamic_index_in_dim(
            up_weight.reshape(depth, shards, reps, ff_own // shards), rep, 2, keepdims=False
        ).reshape(depth, ff_own)
        down_part = lax.dynamic_slice_in_dim(
            down_weight[0], rep * (ff_own // shards), ff_own // shards, 0
        )

        halves = []
        for part in (heads_part, merge_part, up_part, down_part):
            kept = rows_of_core(part, core)
            other = swap(rows_of_core(part, 1 - core))
            halves.append((jnp.where(on_first, kept, other), jnp.where(on_first, other, kept)))
        for s in range(sections):
            full = [
                lax.all_gather(pair[s], ("shard", "section"), axis=0, tiled=True) for pair in halves
            ]
            if not strided:
                full[1] = lax.dynamic_slice_in_dim(full[1], rep * width, width, 0)
            weights.append(full)

    own_lengths = rows_of_core(doc_lengths, core)
    lengths = jnp.concatenate(gathered_blocks(own_lengths, "rep"), axis=0)
    ends = jnp.cumsum(lengths, axis=1)
    position = jnp.arange(slot_rows, dtype=jnp.int32)
    segment = jnp.sum((position[None, :, None] >= ends[:, None, :]).astype(jnp.int32), axis=2)
    visible = jnp.logical_and(
        segment[:, :, None] == segment[:, None, :], position[None, None, :] <= position[None, :, None]
    ).astype(F32)
    slot_count = reps * slots

    own_tokens = rows_of_core(tokens, core)
    own_cotangent = rows_of_core(cotangent, core)
    block_shapes = [sds((n, features))] * reps
    attention_flops = 2 * all_rows * features * 4 * width
    mlp_flops = 4 * all_rows * features * ff_own

    hidden = own_tokens
    normed = call(
        norm_kernel, [sds((n, features))], [hidden, vector(0, 0), vector(0, 1)]
    )[0]
    saved = []
    outputs = []
    for s in range(sections):
        normed_blocks = gathered_blocks(normed, "rep")
        if fast:
            second_pair, _ = mlp_weights(s, other_b if s == 0 else blocks_a[shards - 1])
            weights[s] += list(second_pair)
        wh, wm, wu, wd = weights[s]
        results = call(
            make_attention_forward(reps, head_size),
            [
                sds((all_rows, features)),
                sds((all_rows, 3 * width)),
                sds((slot_count, (width // head_size) * slot_rows, slot_rows), F32),
                sds((all_rows, width)),
            ]
            + block_shapes,
            normed_blocks + [wh, joint_vector(s), visible, wm],
            attention_flops,
        )
        normed_all, joint, probs, attended = results[:4]
        terms = from_peers(results[4:], "rep")
        if fast and s + 1 < sections:
            first_pair, _ = attention_weights(s + 1, blocks_a[shards - 1])
            weights.append(list(first_pair))
        middle, second = call(
            make_middle(reps),
            [sds((n, features), F32), sds((n, features))],
            [hidden] + terms + [vector(s, 4), vector(s, 5), vector(s, 6)],
        )
        results = call(
            make_mlp_forward(reps),
            [sds((all_rows, features)), sds((all_rows, ff_own), F32), sds((all_rows, ff_own))]
            + block_shapes,
            gathered_blocks(second, "rep") + [wu, up_vector(s), wd],
            mlp_flops,
        )
        second_all, before, active = results[:3]
        terms = from_peers(results[3:], "rep")
        saved.append((hidden, normed_all, joint, probs, attended, middle, second_all, before, active))
        if s + 1 < sections:
            hidden, normed = call(
                make_block_end(reps, True),
                [sds((n, features)), sds((n, features))],
                [middle] + terms + [vector(s, 7), vector(s + 1, 0), vector(s + 1, 1)],
            )
            outputs.append(hidden)
        else:
            outputs.append(
                call(
                    make_block_end(reps, False),
                    [sds((n, features))],
                    [middle] + terms + [vector(s, 7)],
                )[0]
            )

    grad_out = own_cotangent
    hidden_grads = [None] * sections
    vector_grads = [None] * sections
    weight_grads = [None] * sections
    tasks = []

    def over_slots(left, right):
        product = t_dot(left, right).astype(LOW)
        return lax.psum_scatter(product, ("shard", "section"), scatter_dimension=0, tiled=True)

    for s in reversed(range(sections)):
        wh, wm, wu, wd = weights[s]
        hidden, normed_all, joint, probs, attended, middle, second_all, before, active = saved[s]
        row = sds((1, features), F32)
        out_blocks = gathered_blocks(grad_out, "rep")
        if tasks:
            out_blocks = window(out_blocks, tasks)
        results = call(
            make_mlp_backward(reps),
            [sds((all_rows, features)), sds((all_rows, ff_own)), sds((1, ff_own), F32)]
            + block_shapes,
            out_blocks + [wd, wu, before],
            mlp_flops,
        )
        down_all, before_all, up_sum = results[:3]
        terms = from_peers(results[3:], "rep")
        if fast:
            piece = sds((features // 2, features))
            flops = 2 * all_rows * features * features
            down_pair = call(
                make_weight_gradient(shards), [piece, piece], [active, down_all], flops, where
            )
            grad_down = GradientSum(down_pair, s, TIE_DOWN, COPY_DOWN)
            terms = window(terms, tasks, [grad_down])
        else:
            grad_down = over_slots(active, down_all)
            grad_up = over_slots(second_all, before_all)
        g_middle, g_merge, second_gain_sum, second_shift_sum, output_sum, down_sum = call(
            make_middle_backward(reps),
            [sds((n, features), F32), sds((n, features))] + [row] * 4,
            [grad_out, middle] + terms + [vector(s, 5)],
        )
        merge_blocks = gathered_blocks(g_merge, "rep")
        if fast:
            up_pair = call(
                make_weight_gradient(shards),
                [piece, piece],
                [second_all, before_all],
                flops,
                after(where, g_merge),
            )
            grad_up = GradientSum(up_pair, s, TIE_UP)
            merge_blocks = window(merge_blocks, tasks, [grad_up])
        results = call(
            make_attention_backward(reps, head_size),
            [
                sds((all_rows, features)),
                sds((all_rows, 3 * width)),
                sds((1, width), F32),
                sds((1, width), F32),
            ]
            + block_shapes,
            merge_blocks + [wm, wh, joint, probs],
            2 * attention_flops,
        )
        merge_all, joint_all, query_sum, value_sum = results[:4]
        terms = from_peers(results[4:], "rep")
        if fast:
            both_pair = call(
                make_attention_gradient(shards),
                [piece, piece],
                [normed_all, joint_all, attended, merge_all],
                flops,
                where,
            )
            grad_heads, grad_merge = GradientSum(both_pair, s), None
            terms = window(terms, tasks, [grad_heads])
        elif strided:
            grad_heads = over_slots(normed_all, joint_all)
            grad_merge = over_slots(attended, merge_all)
        else:
            grad_heads = over_slots(normed_all, joint_all)
            product = t_dot(attended, merge_all).astype(LOW)
            spread = lax.dynamic_update_slice_in_dim(
                jnp.zeros((features, features), LOW), product, rep * width, 0
            )
            grad_merge = lax.psum_scatter(
                spread, ("shard", "section"), scatter_dimension=0, tiled=True
            )
        grad_out, first_gain_sum, first_shift_sum = call(
            make_first_backward(reps),
            [sds((n, features)), row, row],
            [g_middle, hidden] + terms + [vector(s, 0)],
        )
        hidden_grads[s] = grad_out

        def placed_heads(part):
            if strided:
                wide = jnp.zeros((shards, reps, head_run), F32)
                part = part.reshape(shards, 1, head_run)
                return lax.dynamic_update_slice_in_dim(wide, part, rep, 1).reshape(shards, 1, depth)
            wide = jnp.zeros((reps, width), F32)
            return lax.dynamic_update_slice_in_dim(wide, part, rep, 0).reshape(shards, 1, depth)

        wide_up = lax.dynamic_update_slice_in_dim(
            jnp.zeros((shards, reps, ff_own // shards), F32),
            up_sum.reshape(shards, 1, ff_own // shards),
            rep,
            1,
        ).reshape(shards, -1, depth)
        vector_grads[s] = jnp.concatenate(
            [
                first_gain_sum.reshape(shards, 1, depth),
                first_shift_sum.reshape(shards, 1, depth),
                placed_heads(query_sum),
                placed_heads(value_sum),
                output_sum.reshape(shards, 1, depth),
                second_gain_sum.reshape(shards, 1, depth),
                second_shift_sum.reshape(shards, 1, depth),
                down_sum.reshape(shards, 1, depth),
                wide_up,
            ],
            axis=1,
        )
        weight_grads[s] = (grad_heads, grad_merge, grad_up, grad_down)

    own_sum = jnp.where(on_first, vector_grads[0], vector_grads[1])
    other_sum = jnp.where(on_first, vector_grads[1], vector_grads[0])
    own_sum = own_sum + swap(other_sum)
    pieces = from_peers(
        [
            lax.dynamic_index_in_dim(own_sum, shard ^ k, 0, keepdims=False)
            for k in range(shards)
        ],
        "shard",
    )
    total = sum(pieces[1:], pieces[0])
    pieces = gathered_blocks(total, "rep")
    total = sum(pieces[1:], pieces[0])
    singles = [total[number].reshape(1, depth) for number in range(8)]
    grad_up_bias = total[8:].reshape(1, -1)

    def owned(number):
        parts = []
        for s in range(sections):
            mine = weight_grads[s][number]
            theirs = lax.ppermute(mine, "section", [(1 - s, s)])
            parts.append(jnp.concatenate([mine, theirs] if s == 0 else [theirs, mine], axis=0))
        return parts

    def over_reps(number):
        parts = owned(number)
        lists = [gathered_blocks(parts[s], "rep", s) for s in range(sections)]
        return [jnp.where(on_first, a, b) for a, b in zip(*lists)]

    if fast:

        def both_sections(number):
            return [p for s in range(sections) for p in weight_grads[s][number].finish()]

        grad_up = call(
            make_place_up(reps), [sds((depth, ff), F32)], both_sections(2), scalars=where
        )[0][None]
        grad_down = call(
            make_place_down(reps),
            [sds((ff // shards, features), F32)],
            both_sections(3),
            scalars=where,
        )[0][None]
        lane = jnp.arange(head_run, dtype=jnp.int32)[:, None]
        column = jnp.arange(reps * head_run, dtype=jnp.int32)[None, :]
        places = jnp.stack(
            [(column == (rep ^ k) * head_run + lane).astype(LOW) for k in range(reps)]
        )
        grad_heads, grad_merge = call(
            make_place_attention(reps),
            [sds((depth, 3 * features), F32), sds((depth, features), F32)],
            both_sections(0) + [places],
            scalars=where,
        )
        grad_heads, grad_merge = grad_heads[None], grad_merge[None]
    else:
        heads_pieces = over_reps(0)
        if strided:
            lane = jnp.arange(head_run, dtype=jnp.int32)[:, None]
            place = jnp.arange(reps * head_run, dtype=jnp.int32)[None, :]
            places = jnp.stack(
                [(place == (rep ^ k) * head_run + lane).astype(LOW) for k in range(reps)]
            )
            grad_heads = call(
                make_spread_columns(reps),
                [sds((depth, 3 * features), F32)],
                heads_pieces + [places],
            )[0][None]
            merge_pieces = over_reps(1)
            grad_merge = jnp.zeros((reps, head_run, features), F32)
            for k, piece in enumerate(merge_pieces):
                grad_merge = lax.dynamic_update_slice_in_dim(
                    grad_merge, piece.astype(F32)[None], rep ^ k, 0
                )
            grad_merge = grad_merge.reshape(1, depth, features)
        else:
            grad_heads = jnp.zeros((depth, 3, reps, width), F32)
            for k, piece in enumerate(heads_pieces):
                grad_heads = lax.dynamic_update_slice_in_dim(
                    grad_heads, piece.astype(F32).reshape(depth, 3, 1, width), rep ^ k, 2
                )
            grad_heads = grad_heads.reshape(1, depth, 3 * features)
            parts = owned(1)
            grad_merge = lax.psum(jnp.where(on_first, parts[0], parts[1]), "rep").astype(F32)[None]

        grad_up = jnp.zeros((depth, shards, reps, ff_own // shards), F32)
        for k, piece in enumerate(over_reps(2)):
            grad_up = lax.dynamic_update_slice_in_dim(
                grad_up, piece.astype(F32).reshape(depth, shards, 1, ff_own // shards), rep ^ k, 2
            )
        grad_up = grad_up.reshape(1, depth, ff)
        grad_down = jnp.zeros((reps, ff_own // shards, features), F32)
        for k, piece in enumerate(over_reps(3)):
            grad_down = lax.dynamic_update_slice_in_dim(
                grad_down, piece.astype(F32)[None], rep ^ k, 0
            )
        grad_down = grad_down.reshape(1, ff // shards, features)

    def by_section(pair):
        own = jnp.where(on_first, pair[0], pair[1])
        other = swap(jnp.where(on_first, pair[1], pair[0]))
        return jnp.concatenate(
            [jnp.where(on_first, own, other), jnp.where(on_first, other, own)], axis=0
        )[None]

    activations = by_section(outputs)
    input_grads = by_section(hidden_grads)
    (
        grad_first_gain,
        grad_first_shift,
        grad_query,
        grad_value,
        grad_output,
        grad_second_gain,
        grad_second_shift,
        grad_down_bias,
    ) = singles
    return (
        activations,
        input_grads,
        grad_heads,
        grad_merge,
        grad_up,
        grad_down,
        grad_first_gain,
        grad_first_shift,
        grad_query,
        grad_value,
        grad_output,
        grad_second_gain,
        grad_second_shift,
        grad_up_bias,
        grad_down_bias,
    )


def solution(mesh):
    rows = P(("shard", "rep"), None)
    matrix = P("section", "shard", None)
    line = P("section", "shard")
    return jax.shard_map(
        body,
        mesh=mesh,
        in_specs=(rows, rows) + (matrix,) * 4 + (line,) * 9 + (rows,),
        out_specs=(P("section", ("shard", "rep"), None),) * 2 + (matrix,) * 4 + (line,) * 9,
        check_vma=False,
    )
```

```python
import math

import jax
import jax.numpy as jnp
from jax import lax
from jax.experimental import pallas as pl
from jax.experimental.pallas import tpu as pltpu
from jax.sharding import PartitionSpec as P

HEADS = 16
TIE_MLP = 4
NORM_EPS = 1e-05
GELU_COEF = 0.7978845608028654
GELU_CUBE = 0.044715
LOW = jnp.bfloat16
F32 = jnp.float32


def dot(left, right):
    return jnp.dot(left, right, preferred_element_type=F32)


def dot_t(left, right):
    return lax.dot_general(left, right, (((1,), (1,)), ((), ())), preferred_element_type=F32)


def t_dot(left, right):
    return lax.dot_general(left, right, (((0,), (0,)), ((), ())), preferred_element_type=F32)


def call(kernel, outs, args, flops=0, scalars=None):
    nbytes = sum(a.size * a.dtype.itemsize for a in args) + sum(
        math.prod(o.shape) * jnp.dtype(o.dtype).itemsize for o in outs
    )
    vmem = pl.BlockSpec(memory_space=pltpu.VMEM)
    return pl.pallas_call(
        kernel,
        out_shape=outs,
        in_specs=[pl.BlockSpec(memory_space=pltpu.SMEM)] * (scalars is not None)
        + [vmem] * len(args),
        out_specs=[vmem] * len(outs),
        compiler_params=pltpu.CompilerParams(vmem_limit_bytes=40 * 2**20),
        cost_estimate=pl.CostEstimate(flops=flops, bytes_accessed=nbytes, transcendentals=0),
    )(*(([] if scalars is None else [scalars]) + list(args)))


def sds(shape, dtype=LOW):
    return jax.ShapeDtypeStruct(shape, dtype)


def normalized(rows):
    centred = rows - jnp.mean(rows, axis=-1, keepdims=True)
    spread = jnp.mean(centred * centred, axis=-1, keepdims=True)
    rstd = lax.rsqrt(spread + NORM_EPS)
    return centred * rstd, rstd


def affine(xhat, gain_ref, shift_ref):
    return (xhat * gain_ref[...].astype(F32) + shift_ref[...].astype(F32)).astype(LOW)


def column_sum(rows):
    return jnp.sum(rows, axis=0, keepdims=True)


def joined(refs):
    return jnp.concatenate([ref[...] for ref in refs], axis=0)


def added(refs):
    total = refs[0][...].astype(F32)
    for ref in refs[1:]:
        total = total + ref[...].astype(F32)
    return total


def store_blocks(refs, rows):
    size = refs[0].shape[0]
    for number, ref in enumerate(refs):
        ref[...] = rows[number * size : (number + 1) * size].astype(ref.dtype)


def norm_kernel(rows_ref, gain_ref, shift_ref, out_ref):
    xhat, _ = normalized(rows_ref[...].astype(F32))
    out_ref[...] = affine(xhat, gain_ref, shift_ref)


def head_masks(width, head_size):
    lane = lax.broadcasted_iota(jnp.int32, (1, width), 1)
    return [
        jnp.logical_and(lane >= h * head_size, lane < (h + 1) * head_size).astype(F32)
        for h in range(width // head_size)
    ]


def stacked_heads(rows, masks):
    wide = rows.astype(F32)
    return jnp.concatenate([(wide * m).astype(LOW) for m in masks], axis=0)


def folded_heads(stacked, masks):
    size = stacked.shape[0] // len(masks)
    total = stacked[:size] * masks[0]
    for h in range(1, len(masks)):
        total = total + stacked[h * size : (h + 1) * size] * masks[h]
    return total


def make_attention_forward(parts, head_size):
    scale = 1.0 / math.sqrt(head_size)

    def kernel(*refs):
        x_refs, (wh, jb, vis, wm) = refs[:parts], refs[parts : parts + 4]
        x_all, joint, probs, attended = refs[parts + 4 : parts + 8]
        blocks = refs[parts + 8 :]
        rows = joined(x_refs)
        x_all[...] = rows
        joint[...] = (dot(rows, wh[...]) + jb[...].astype(F32)).astype(LOW)
        width = wm.shape[0]
        masks = head_masks(width, head_size)
        slots, size, _ = vis.shape
        for b in range(slots):
            at = slice(b * size, (b + 1) * size)
            query = stacked_heads(joint[at, :width], masks)
            scores = dot_t(query, joint[at, width : 2 * width]) * scale
            seen = jnp.concatenate([vis[b]] * len(masks), axis=0) > 0.0
            scores = jnp.where(seen, scores, -1e30)
            top = jnp.max(scores, axis=-1, keepdims=True)
            weights = jnp.exp(scores - top)
            share = weights * (1.0 / jnp.sum(weights, axis=-1, keepdims=True))
            probs[b] = share
            mixed = dot(share.astype(LOW), joint[at, 2 * width :])
            attended[at, :] = folded_heads(mixed, masks).astype(LOW)
        store_blocks(blocks, dot(attended[...], wm[...]))

    return kernel


def make_attention_backward(parts, head_size):
    scale = 1.0 / math.sqrt(head_size)

    def kernel(*refs):
        g_refs, (wm, wh, joint, probs) = refs[:parts], refs[parts : parts + 4]
        g_all, g_joint, g_query, g_value = refs[parts + 4 : parts + 8]
        blocks = refs[parts + 8 :]
        rows = joined(g_refs)
        g_all[...] = rows
        g_attended = dot_t(rows, wm[...]).astype(LOW)
        width = wm.shape[0]
        masks = head_masks(width, head_size)
        slots, _, size = probs.shape
        for b in range(slots):
            at = slice(b * size, (b + 1) * size)
            query = stacked_heads(joint[at, :width], masks)
            g_heads = stacked_heads(g_attended[at], masks)
            share = probs[b]
            g_probs = dot_t(g_heads, joint[at, 2 * width :])
            inner = jnp.sum(share * g_probs, axis=-1, keepdims=True)
            g_scores = (share * (g_probs - inner)).astype(LOW)
            g_q = folded_heads(dot(g_scores, joint[at, width : 2 * width]), masks) * scale
            g_joint[at, :width] = g_q.astype(LOW)
            g_joint[at, width : 2 * width] = (t_dot(g_scores, query) * scale).astype(LOW)
            g_joint[at, 2 * width :] = t_dot(share.astype(LOW), g_heads).astype(LOW)
        store_blocks(blocks, dot_t(g_joint[...], wh[...]))
        g_query[...] = column_sum(g_joint[:, :width].astype(F32))
        g_value[...] = column_sum(g_joint[:, 2 * width :].astype(F32))

    return kernel


def make_middle(parts):
    def kernel(hidden, *refs):
        terms, (bias, gain, shift) = refs[:parts], refs[parts : parts + 3]
        middle, second = refs[parts + 3 :]
        rows = hidden[...].astype(F32) + added(terms) + bias[...].astype(F32)
        middle[...] = rows
        xhat, _ = normalized(rows)
        second[...] = affine(xhat, gain, shift)

    return kernel


def make_block_end(parts, with_norm):
    def kernel(middle, *refs):
        terms, bias = refs[:parts], refs[parts]
        rest = refs[parts + 1 :]
        rows = (middle[...] + added(terms) + bias[...].astype(F32)).astype(LOW)
        if with_norm:
            gain, shift, out, normed = rest
            xhat, _ = normalized(rows.astype(F32))
            normed[...] = affine(xhat, gain, shift)
        else:
            (out,) = rest
        out[...] = rows

    return kernel


def make_mlp_forward(parts):
    def kernel(*refs):
        x_refs, (wu, ub, wd) = refs[:parts], refs[parts : parts + 3]
        x_all, before, active = refs[parts + 3 : parts + 6]
        blocks = refs[parts + 6 :]
        rows = joined(x_refs)
        x_all[...] = rows
        value = dot(rows, wu[...]) + ub[...].astype(F32)
        before[...] = value
        inner = jnp.tanh(GELU_COEF * (value + GELU_CUBE * value * value * value))
        active[...] = (0.5 * value * (1.0 + inner)).astype(LOW)
        if blocks:
            store_blocks(blocks, dot(active[...], wd[...]))

    return kernel


def make_mlp_backward(parts):
    def kernel(*refs):
        g_refs, (wd, wu, before) = refs[:parts], refs[parts : parts + 3]
        g_all, g_before, g_bias = refs[parts + 3 : parts + 6]
        blocks = refs[parts + 6 :]
        rows = joined(g_refs)
        g_all[...] = rows
        g_active = dot_t(rows, wd[...])
        value = before[...]
        inner = jnp.tanh(GELU_COEF * (value + GELU_CUBE * value * value * value))
        slope = 0.5 * (1.0 + inner) + 0.5 * value * (1.0 - inner * inner) * GELU_COEF * (
            1.0 + 3.0 * GELU_CUBE * value * value
        )
        result = (g_active * slope).astype(LOW)
        g_before[...] = result
        g_bias[...] = column_sum(result.astype(F32))
        store_blocks(blocks, dot_t(result, wu[...]))

    return kernel


def norm_back(grad, xhat, rstd, gain_ref):
    e = grad * gain_ref[...].astype(F32)
    mean_e = jnp.mean(e, axis=-1, keepdims=True)
    mean_ex = jnp.mean(e * xhat, axis=-1, keepdims=True)
    return rstd * (e - mean_e - xhat * mean_ex)


def make_middle_backward(parts):
    def kernel(grad_out, middle, *refs):
        terms, gain = refs[:parts], refs[parts]
        g_middle, g_merge, g_gain, g_shift, g_output, g_down = refs[parts + 1 :]
        grad = added(terms)
        xhat, rstd = normalized(middle[...])
        own = grad_out[...].astype(F32)
        rows = own + norm_back(grad, xhat, rstd, gain)
        g_middle[...] = rows
        low_rows = rows.astype(LOW)
        g_merge[...] = low_rows
        g_gain[...] = column_sum(grad * xhat)
        g_shift[...] = column_sum(grad)
        g_output[...] = column_sum(low_rows.astype(F32))
        g_down[...] = column_sum(own)

    return kernel


def make_first_backward(parts):
    def kernel(g_middle, hidden, *refs):
        terms, gain = refs[:parts], refs[parts]
        g_hidden, g_gain, g_shift = refs[parts + 1 :]
        grad = added(terms)
        xhat, rstd = normalized(hidden[...].astype(F32))
        g_hidden[...] = (g_middle[...] + norm_back(grad, xhat, rstd, gain)).astype(LOW)
        g_gain[...] = column_sum(grad * xhat)
        g_shift[...] = column_sum(grad)

    return kernel


def pick_columns_kernel(matrix, left, right, out):
    block = left.shape[0]
    step = left.shape[1]
    for m in range(out.shape[1] // step):
        first = dot(matrix[:, 2 * m * block : (2 * m + 1) * block], left[...])
        second = dot(matrix[:, (2 * m + 1) * block : (2 * m + 2) * block], right[...])
        out[:, m * step : (m + 1) * step] = (first + second).astype(LOW)


def make_spread_columns(parts):
    def kernel(*refs):
        pieces, place, out = refs[:parts], refs[parts], refs[parts + 1]
        size = place.shape[1]
        wide = place.shape[2]
        for m in range(out.shape[1] // wide):
            total = dot(pieces[0][:, m * size : (m + 1) * size], place[0])
            for k in range(1, parts):
                total = total + dot(pieces[k][:, m * size : (m + 1) * size], place[k])
            out[:, m * wide : (m + 1) * wide] = total

    return kernel


def at_block(index, size):
    return pl.ds(pl.multiple_of(index * size, size), size)


def prepare_attention_kernel(where, heads, merge, left, right, kept, sent):
    core, rep = where[0], where[1]
    block, step = left.shape
    run = step // 2
    half = kept.shape[0]
    width = kept.shape[1] // 4
    packed = []
    for m in range(3 * width // step):
        first = dot(heads[:, 2 * m * block : (2 * m + 1) * block], left[...])
        second = dot(heads[:, (2 * m + 1) * block : (2 * m + 2) * block], right[...])
        packed.append((first + second).astype(LOW))
    own = merge[at_block(rep, run), :]
    packed.append(
        jnp.concatenate(
            [own[:, j * width : (j + 1) * width] for j in range(2 * half // run)], axis=0
        )
    )
    rows = jnp.concatenate(packed, axis=1)
    first = core == 0
    kept[...] = jnp.where(first, rows[:half], rows[half:])
    sent[...] = jnp.where(first, rows[half:], rows[:half])


def prepare_mlp_kernel(where, up, down, kept, sent):
    core, rep = where[0], where[1]
    half = kept.shape[0] // 2
    ff_own = kept.shape[1]
    run = 2 * half
    reps = up.shape[1] // ff_own
    for target, which in ((kept, core), (sent, 1 - core)):
        rows = at_block(which, half)
        for m in range(ff_own // run):
            target[:half, m * run : (m + 1) * run] = up[rows, at_block(m * reps + rep, run)]
        target[half:, :] = down[at_block(2 * rep + which, half), :]


def make_assemble_attention(shards):
    def kernel(where, *refs):
        core, shard = where[0], where[2]
        heads, merge = refs[2 * shards :]
        half = refs[0].shape[0]
        width = merge.shape[0]
        run = width // shards
        for number, ref in enumerate(refs[: 2 * shards]):
            source = lax.rem(shard - number % shards + shards, shards)
            which = core if number < shards else 1 - core
            heads[at_block(2 * source + which, half), :] = ref[:, : 3 * width]
            for j in range(half // run):
                merge[at_block(source, run), at_block(which * (half // run) + j, width)] = ref[
                    j * run : (j + 1) * run, 3 * width :
                ]

    return kernel


def make_assemble_mlp(shards):
    def kernel(where, *refs):
        core, shard = where[0], where[2]
        up, down = refs[2 * shards :]
        half = refs[0].shape[0] // 2
        for number, ref in enumerate(refs[: 2 * shards]):
            source = lax.rem(shard - number % shards + shards, shards)
            which = core if number < shards else 1 - core
            rows = at_block(2 * source + which, half)
            up[rows, :] = ref[:half, :]
            down[rows, :] = ref[half:, :]

    return kernel


def split_by_core(core, product, kept, sent, shards, offset=0):
    half = product.shape[0] // (2 * shards)
    stride = kept.shape[0] // shards
    first = core == 0
    for b in range(shards):
        one = product[2 * b * half : (2 * b + 1) * half]
        two = product[(2 * b + 1) * half : (2 * b + 2) * half]
        at = slice(b * stride + offset, b * stride + offset + half)
        kept[at, : one.shape[1]] = jnp.where(first, one, two)
        sent[at, : one.shape[1]] = jnp.where(first, two, one)


def make_mlp_gradient(shards):
    def kernel(where, active, down, second, before, kept, sent):
        core = where[0]
        half = kept.shape[0] // shards // 2
        product = t_dot(active[...], down[...]).astype(LOW)
        split_by_core(core, product, kept, sent, shards, 0)
        product = t_dot(second[...], before[...]).astype(LOW)
        split_by_core(core, product, kept, sent, shards, half)

    return kernel


def make_attention_gradient(shards):
    def kernel(where, normed, joint, attended, merge, kept, sent):
        core = where[0]
        split_by_core(core, t_dot(normed[...], joint[...]).astype(LOW), kept, sent, shards)
        product = t_dot(attended[...], merge[...]).astype(LOW)
        width = product.shape[0]
        run = width // shards
        half = kept.shape[0] // shards
        count = half // run
        first = core == 0
        for b in range(shards):
            rows = product[b * run : (b + 1) * run]
            for j in range(count):
                one = rows[:, j * width : (j + 1) * width]
                two = rows[:, (count + j) * width : (count + j + 1) * width]
                at = slice(b * half + j * run, b * half + (j + 1) * run)
                kept[at, 3 * width :] = jnp.where(first, one, two)
                sent[at, 3 * width :] = jnp.where(first, two, one)

    return kernel


def chosen(core, refs, number, count):
    return jnp.where(core == 0, refs[number][...], refs[count + number][...])


def make_place_attention(parts):
    def kernel(where, *refs):
        core, rep = where[0], where[1]
        place, heads, merge = refs[2 * parts :]
        run = place.shape[1]
        wide = place.shape[2]
        width = heads.shape[1] // (3 * parts)
        pieces = [chosen(core, refs, k, parts) for k in range(parts)]
        for m in range(heads.shape[1] // wide):
            total = dot(pieces[0][:, m * run : (m + 1) * run], place[0])
            for k in range(1, parts):
                total = total + dot(pieces[k][:, m * run : (m + 1) * run], place[k])
            heads[:, m * wide : (m + 1) * wide] = total
        for k in range(parts):
            for j in range(pieces[k].shape[0] // run):
                merge[at_block(jnp.bitwise_xor(rep, k), run), j * width : (j + 1) * width] = pieces[
                    k
                ][j * run : (j + 1) * run, 3 * width :].astype(F32)

    return kernel


def make_place_mlp(parts):
    def kernel(where, *refs):
        core, rep = where[0], where[1]
        up, down = refs[2 * parts :]
        run = up.shape[0]
        half = run // 2
        for k in range(parts):
            piece = chosen(core, refs, k, parts).astype(F32)
            peer = jnp.bitwise_xor(rep, k)
            for c in range(2):
                start = 2 * c * half
                down[at_block(2 * peer + c, half), :] = piece[start : start + half]
                for m in range(piece.shape[1] // run):
                    up[c * half : (c + 1) * half, at_block(m * parts + peer, run)] = piece[
                        start + half : start + 2 * half, m * run : (m + 1) * run
                    ]

    return kernel


def swap(block):
    return lax.ppermute(block, "section", [(0, 1), (1, 0)])


def from_peers(blocks, axis, section=None):
    count = lax.axis_size(axis)
    received = []
    for k in range(1, count):
        if section is None:
            pairs = [(i, i ^ k) for i in range(count)]
            received.append(lax.ppermute(blocks[k], axis, pairs))
        else:
            pairs = [(section * count + i, section * count + (i ^ k)) for i in range(count)]
            received.append(lax.ppermute(blocks[k], ("section", axis), pairs))
    return [blocks[0]] + received


def after(value, other):
    return lax.optimization_barrier((value, other))[0]


def ring_gather(block):
    count = lax.axis_size("shard")
    blocks = [block]
    for _ in range(count - 1):
        blocks.append(
            lax.ppermute(blocks[-1], "shard", [(i, (i + 1) % count) for i in range(count)])
        )
    return blocks + [swap(b) for b in blocks]


class GradientSum:
    def __init__(self, pair, section, tie=None, copy=None, direct=False):
        self.direct = direct
        self.section, self.tie, self.copy, self.age = section, tie, copy, 0
        self.state, self.stage = list(pair), 0

    def advance(self):
        self.age += 1
        if self.age in (1, self.tie, self.copy):
            self.next_stage()
            return True
        return False

    def next_stage(self):
        self.stage += 1
        s = self.section
        if self.stage == 1:
            kept, arrived = self.state[0], swap(self.state[1])
            self.state = (kept.astype(F32) + arrived.astype(F32)).astype(LOW)
        elif self.stage == 2 and self.direct:
            count, shard = lax.axis_size("shard"), lax.axis_index("shard")
            size = self.state.shape[0] // count
            pieces = from_peers(
                [
                    lax.dynamic_slice_in_dim(self.state, (shard ^ k) * size, size, 0)
                    for k in range(count)
                ],
                "shard",
            )
            pieces = [p.astype(F32) for p in pieces]
            self.state = sum(pieces[1:], pieces[0]).astype(LOW)
        elif self.stage == 2:
            self.state = lax.psum_scatter(self.state, "shard", scatter_dimension=0, tiled=True)
        elif self.stage == 3:
            theirs = lax.ppermute(self.state, "section", [(1 - s, s)])
            order = [self.state, theirs] if s == 0 else [theirs, self.state]
            self.state = jnp.concatenate(order, axis=0)
        elif self.stage == 4:
            self.state = gathered_blocks(self.state, "rep", s)

    def finish(self):
        while self.stage < 4:
            self.next_stage()
        return self.state


def window(waiting, tasks, new=()):
    tied = [task for task in tasks if task.advance()] + list(new)
    tasks.extend(new)
    waiting, states = lax.optimization_barrier((waiting, [task.state for task in tied]))
    for task, state in zip(tied, states):
        task.state = state
    return waiting


def gathered_blocks(block, axis, section=None):
    return from_peers([block] * lax.axis_size(axis), axis, section)


def body(
    tokens,
    doc_lengths,
    heads_weight,
    merge_weight,
    up_weight,
    down_weight,
    first_gain,
    first_shift,
    query_bias,
    value_bias,
    output_bias,
    second_gain,
    second_shift,
    up_bias,
    down_bias,
    cotangent,
):
    sections = lax.axis_size("section")
    shards = lax.axis_size("shard")
    reps = lax.axis_size("rep")
    assert sections == 2
    core = lax.axis_index("section")
    shard = lax.axis_index("shard")
    rep = lax.axis_index("rep")
    on_first = core == 0

    features = tokens.shape[1]
    slot_rows = tokens.shape[0] // doc_lengths.shape[0]
    slots = doc_lengths.shape[0] // sections
    n = slots * slot_rows
    all_rows = reps * n
    head_size = features // HEADS
    width = features // reps
    ff = up_weight.shape[2]
    ff_own = ff // reps
    depth = features // shards
    strided = HEADS % (shards * reps) == 0
    head_run = (HEADS // (shards * reps)) * head_size if strided else width
    fast = strided and depth == reps * head_run and (ff_own // shards) == depth
    fast = fast and ff_own == features and depth % 256 == 0 and width == depth
    where = jnp.stack([core, rep, shard]).astype(jnp.int32)

    def rows_of_core(array, which):
        return lax.dynamic_index_in_dim(
            array.reshape((sections, array.shape[0] // sections) + array.shape[1:]),
            which,
            0,
            keepdims=False,
        )

    vectors = (
        first_gain,
        first_shift,
        query_bias,
        value_bias,
        output_bias,
        second_gain,
        second_shift,
        down_bias,
        up_bias,
    )
    packed = jnp.concatenate([v.reshape(-1, depth) for v in vectors], axis=0)
    vector_rows = packed.shape[0]
    shard_order = gathered_blocks(packed, "shard")

    def in_order(pieces, index):
        count = len(pieces)
        result = []
        for j in range(count):
            total = pieces[0]
            for k in range(1, count):
                total = jnp.where(index == (j ^ k), pieces[k], total)
            result.append(total)
        return jnp.stack(result)

    own_vectors = in_order(shard_order, shard)
    other_vectors = swap(own_vectors)
    section_vectors = (
        jnp.where(on_first, own_vectors, other_vectors),
        jnp.where(on_first, other_vectors, own_vectors),
    )

    def vector(s, number):
        return section_vectors[s][:, number, :].reshape(1, features)

    def own_heads_part(flat):
        if strided:
            cut = flat.reshape(shards, reps, head_run)
            return lax.dynamic_index_in_dim(cut, rep, 1, keepdims=False).reshape(1, width)
        return lax.dynamic_index_in_dim(flat.reshape(reps, width), rep, 0, keepdims=False).reshape(
            1, width
        )

    def up_vector(s):
        flat = section_vectors[s][:, 8:, :].reshape(shards, reps, ff_own // shards)
        return lax.dynamic_index_in_dim(flat, rep, 1, keepdims=False).reshape(1, ff_own)

    def joint_vector(s):
        query = own_heads_part(vector(s, 2))
        value = own_heads_part(vector(s, 3))
        return jnp.concatenate([query, jnp.zeros_like(query), value], axis=1)

    weights = []
    if fast:
        lane = jnp.arange(reps * head_run, dtype=jnp.int32)[:, None]
        column = jnp.arange(2 * head_run, dtype=jnp.int32)[None, :]
        hit = lane == rep * head_run + column % head_run
        left = jnp.logical_and(hit, column < head_run).astype(LOW)
        right = jnp.logical_and(hit, column >= head_run).astype(LOW)
        half = sds((depth // 2, 4 * width))
        kept_a, sent_a = call(
            prepare_attention_kernel,
            [half, half],
            [heads_weight[0], merge_weight[0], left, right],
            scalars=where,
        )
        whole = sds((depth, ff_own))
        other_a = swap(sent_a)
        kept_b, sent_b = call(
            prepare_mlp_kernel,
            [whole, whole],
            [up_weight[0], down_weight[0]],
            scalars=after(where, other_a),
        )
        other_b = swap(sent_b)

    def attention_weights(s, then):
        mine = on_first if s == 0 else jnp.logical_not(on_first)
        blocks = ring_gather(after(jnp.where(mine, kept_a, other_a), then))
        outs = [sds((features, 3 * width)), sds((width, features))]
        return call(make_assemble_attention(shards), outs, blocks, scalars=where), blocks

    def mlp_weights(s, then):
        mine = on_first if s == 0 else jnp.logical_not(on_first)
        blocks = ring_gather(after(jnp.where(mine, kept_b, other_b), then))
        outs = [sds((features, ff_own)), sds((ff_own, features))]
        return call(make_assemble_mlp(shards), outs, blocks, scalars=where), blocks

    if fast:
        first_pair, blocks_a = attention_weights(0, other_a)
        weights.append(list(first_pair))
    else:
        if strided:
            lane = jnp.arange(reps * head_run, dtype=jnp.int32)[:, None]
            place = jnp.arange(2 * head_run, dtype=jnp.int32)[None, :]
            hit = lane == rep * head_run + place % head_run
            left = jnp.logical_and(hit, place < head_run).astype(LOW)
            right = jnp.logical_and(hit, place >= head_run).astype(LOW)
            heads_part = call(
                pick_columns_kernel, [sds((depth, 3 * width))], [heads_weight[0], left, right]
            )[0]
            merge_part = lax.dynamic_slice_in_dim(merge_weight[0], rep * head_run, head_run, 0)
        else:
            heads_part = lax.dynamic_index_in_dim(
                heads_weight.reshape(depth, 3, reps, width), rep, 2, keepdims=False
            ).reshape(depth, 3 * width)
            merge_part = merge_weight[0]
        up_part = lax.dynamic_index_in_dim(
            up_weight.reshape(depth, shards, reps, ff_own // shards), rep, 2, keepdims=False
        ).reshape(depth, ff_own)
        down_part = lax.dynamic_slice_in_dim(
            down_weight[0], rep * (ff_own // shards), ff_own // shards, 0
        )

        halves = []
        for part in (heads_part, merge_part, up_part, down_part):
            kept = rows_of_core(part, core)
            other = swap(rows_of_core(part, 1 - core))
            halves.append((jnp.where(on_first, kept, other), jnp.where(on_first, other, kept)))
        for s in range(sections):
            full = [
                lax.all_gather(pair[s], ("shard", "section"), axis=0, tiled=True) for pair in halves
            ]
            if not strided:
                full[1] = lax.dynamic_slice_in_dim(full[1], rep * width, width, 0)
            weights.append(full)

    own_lengths = rows_of_core(doc_lengths, core)
    lengths = jnp.concatenate(gathered_blocks(own_lengths, "rep"), axis=0)
    ends = jnp.cumsum(lengths, axis=1)
    position = jnp.arange(slot_rows, dtype=jnp.int32)
    segment = jnp.sum((position[None, :, None] >= ends[:, None, :]).astype(jnp.int32), axis=2)
    visible = jnp.logical_and(
        segment[:, :, None] == segment[:, None, :], position[None, None, :] <= position[None, :, None]
    ).astype(F32)
    slot_count = reps * slots

    own_tokens = rows_of_core(tokens, core)
    own_cotangent = rows_of_core(cotangent, core)
    block_shapes = [sds((n, features))] * reps
    attention_flops = 2 * all_rows * features * 4 * width
    mlp_flops = 4 * all_rows * features * ff_own

    hidden = own_tokens
    normed = call(
        norm_kernel, [sds((n, features))], [hidden, vector(0, 0), vector(0, 1)]
    )[0]
    saved = []
    outputs = []
    for s in range(sections):
        normed_blocks = gathered_blocks(normed, "rep")
        if fast:
            second_pair, _ = mlp_weights(s, other_b if s == 0 else blocks_a[shards - 1])
            weights[s] += list(second_pair)
        wh, wm, wu, wd = weights[s]
        results = call(
            make_attention_forward(reps, head_size),
            [
                sds((all_rows, features)),
                sds((all_rows, 3 * width)),
                sds((slot_count, (width // head_size) * slot_rows, slot_rows), F32),
                sds((all_rows, width)),
            ]
            + block_shapes,
            normed_blocks + [wh, joint_vector(s), visible, wm],
            attention_flops,
        )
        normed_all, joint, probs, attended = results[:4]
        terms = from_peers(results[4:], "rep")
        if fast and s + 1 < sections:
            first_pair, _ = attention_weights(s + 1, blocks_a[shards - 1])
            weights.append(list(first_pair))
        middle, second = call(
            make_middle(reps),
            [sds((n, features), F32), sds((n, features))],
            [hidden] + terms + [vector(s, 4), vector(s, 5), vector(s, 6)],
        )
        results = call(
            make_mlp_forward(reps),
            [sds((all_rows, features)), sds((all_rows, ff_own), F32), sds((all_rows, ff_own))]
            + block_shapes,
            gathered_blocks(second, "rep") + [wu, up_vector(s), wd],
            mlp_flops,
        )
        second_all, before, active = results[:3]
        terms = from_peers(results[3:], "rep")
        saved.append((hidden, normed_all, joint, probs, attended, middle, second_all, before, active))
        if s + 1 < sections:
            hidden, normed = call(
                make_block_end(reps, True),
                [sds((n, features)), sds((n, features))],
                [middle] + terms + [vector(s, 7), vector(s + 1, 0), vector(s + 1, 1)],
            )
            outputs.append(hidden)
        else:
            outputs.append(
                call(
                    make_block_end(reps, False),
                    [sds((n, features))],
                    [middle] + terms + [vector(s, 7)],
                )[0]
            )

    grad_out = own_cotangent
    hidden_grads = [None] * sections
    vector_grads = [None] * sections
    weight_grads = [None] * sections
    tasks = []

    def over_slots(left, right):
        product = t_dot(left, right).astype(LOW)
        return lax.psum_scatter(product, ("shard", "section"), scatter_dimension=0, tiled=True)

    for s in reversed(range(sections)):
        wh, wm, wu, wd = weights[s]
        hidden, normed_all, joint, probs, attended, middle, second_all, before, active = saved[s]
        row = sds((1, features), F32)
        out_blocks = gathered_blocks(grad_out, "rep")
        if tasks:
            out_blocks = window(out_blocks, tasks)
        results = call(
            make_mlp_backward(reps),
            [sds((all_rows, features)), sds((all_rows, ff_own)), sds((1, ff_own), F32)]
            + block_shapes,
            out_blocks + [wd, wu, before],
            mlp_flops,
        )
        down_all, before_all, up_sum = results[:3]
        terms = from_peers(results[3:], "rep")
        if fast:
            piece = sds((features // 2, features))
            flops = 2 * all_rows * features * features
            terms = window(terms, tasks)
        else:
            grad_down = over_slots(active, down_all)
            grad_up = over_slots(second_all, before_all)
        g_middle, g_merge, second_gain_sum, second_shift_sum, output_sum, down_sum = call(
            make_middle_backward(reps),
            [sds((n, features), F32), sds((n, features))] + [row] * 4,
            [grad_out, middle] + terms + [vector(s, 5)],
        )
        merge_blocks = gathered_blocks(g_merge, "rep")
        if fast:
            wide = sds((features, features))
            mlp_pair = call(
                make_mlp_gradient(shards),
                [wide, wide],
                [active, down_all, second_all, before_all],
                2 * flops,
                after(where, g_merge),
            )
            grad_up, grad_down = GradientSum(mlp_pair, s, TIE_MLP, TIE_MLP + 1), None
            merge_blocks = window(merge_blocks, tasks, [grad_up])
        results = call(
            make_attention_backward(reps, head_size),
            [
                sds((all_rows, features)),
                sds((all_rows, 3 * width)),
                sds((1, width), F32),
                sds((1, width), F32),
            ]
            + block_shapes,
            merge_blocks + [wm, wh, joint, probs],
            2 * attention_flops,
        )
        merge_all, joint_all, query_sum, value_sum = results[:4]
        terms = from_peers(results[4:], "rep")
        if fast:
            both_pair = call(
                make_attention_gradient(shards),
                [piece, piece],
                [normed_all, joint_all, attended, merge_all],
                flops,
                where,
            )
            grad_heads, grad_merge = GradientSum(both_pair, s, direct=s == 0), None
            terms = window(terms, tasks, [grad_heads])
        elif strided:
            grad_heads = over_slots(normed_all, joint_all)
            grad_merge = over_slots(attended, merge_all)
        else:
            grad_heads = over_slots(normed_all, joint_all)
            product = t_dot(attended, merge_all).astype(LOW)
            spread = lax.dynamic_update_slice_in_dim(
                jnp.zeros((features, features), LOW), product, rep * width, 0
            )
            grad_merge = lax.psum_scatter(
                spread, ("shard", "section"), scatter_dimension=0, tiled=True
            )
        grad_out, first_gain_sum, first_shift_sum = call(
            make_first_backward(reps),
            [sds((n, features)), row, row],
            [g_middle, hidden] + terms + [vector(s, 0)],
        )
        hidden_grads[s] = grad_out
        if fast and s == 0:
            first_gain_sum, first_shift_sum = window([first_gain_sum, first_shift_sum], tasks)

        def placed_heads(part):
            if strided:
                wide = jnp.zeros((shards, reps, head_run), F32)
                part = part.reshape(shards, 1, head_run)
                return lax.dynamic_update_slice_in_dim(wide, part, rep, 1).reshape(shards, 1, depth)
            wide = jnp.zeros((reps, width), F32)
            return lax.dynamic_update_slice_in_dim(wide, part, rep, 0).reshape(shards, 1, depth)

        wide_up = lax.dynamic_update_slice_in_dim(
            jnp.zeros((shards, reps, ff_own // shards), F32),
            up_sum.reshape(shards, 1, ff_own // shards),
            rep,
            1,
        ).reshape(shards, -1, depth)
        vector_grads[s] = jnp.concatenate(
            [
                first_gain_sum.reshape(shards, 1, depth),
                first_shift_sum.reshape(shards, 1, depth),
                placed_heads(query_sum),
                placed_heads(value_sum),
                output_sum.reshape(shards, 1, depth),
                second_gain_sum.reshape(shards, 1, depth),
                second_shift_sum.reshape(shards, 1, depth),
                down_sum.reshape(shards, 1, depth),
                wide_up,
            ],
            axis=1,
        )
        weight_grads[s] = (grad_heads, grad_merge, grad_up, grad_down)

    own_sum = jnp.where(on_first, vector_grads[0], vector_grads[1])
    other_sum = jnp.where(on_first, vector_grads[1], vector_grads[0])
    own_sum = own_sum + swap(other_sum)
    pieces = from_peers(
        [
            lax.dynamic_index_in_dim(own_sum, shard ^ k, 0, keepdims=False)
            for k in range(shards)
        ],
        "shard",
    )
    total = sum(pieces[1:], pieces[0])
    pieces = gathered_blocks(total, "rep")
    total = sum(pieces[1:], pieces[0])
    singles = [total[number].reshape(1, depth) for number in range(8)]
    grad_up_bias = total[8:].reshape(1, -1)

    def owned(number):
        parts = []
        for s in range(sections):
            mine = weight_grads[s][number]
            theirs = lax.ppermute(mine, "section", [(1 - s, s)])
            parts.append(jnp.concatenate([mine, theirs] if s == 0 else [theirs, mine], axis=0))
        return parts

    def over_reps(number):
        parts = owned(number)
        lists = [gathered_blocks(parts[s], "rep", s) for s in range(sections)]
        return [jnp.where(on_first, a, b) for a, b in zip(*lists)]

    if fast:

        def both_sections(number):
            return [p for s in range(sections) for p in weight_grads[s][number].finish()]

        for s in reversed(range(sections)):
            for number in (2, 0):
                task = weight_grads[s][number]
                while task.stage < 2:
                    task.next_stage()
                if s + 1 < sections:
                    task.state = after(task.state, earlier)
                task.finish()
            earlier = [weight_grads[s][number].state for number in (2, 0)]
        grad_up, grad_down = call(
            make_place_mlp(reps),
            [sds((depth, ff), F32), sds((ff // shards, features), F32)],
            both_sections(2),
            scalars=where,
        )
        grad_up, grad_down = grad_up[None], grad_down[None]
        lane = jnp.arange(head_run, dtype=jnp.int32)[:, None]
        column = jnp.arange(reps * head_run, dtype=jnp.int32)[None, :]
        places = jnp.stack(
            [(column == (rep ^ k) * head_run + lane).astype(LOW) for k in range(reps)]
        )
        grad_heads, grad_merge = call(
            make_place_attention(reps),
            [sds((depth, 3 * features), F32), sds((depth, features), F32)],
            both_sections(0) + [places],
            scalars=where,
        )
        grad_heads, grad_merge = grad_heads[None], grad_merge[None]
    else:
        heads_pieces = over_reps(0)
        if strided:
            lane = jnp.arange(head_run, dtype=jnp.int32)[:, None]
            place = jnp.arange(reps * head_run, dtype=jnp.int32)[None, :]
            places = jnp.stack(
                [(place == (rep ^ k) * head_run + lane).astype(LOW) for k in range(reps)]
            )
            grad_heads = call(
                make_spread_columns(reps),
                [sds((depth, 3 * features), F32)],
                heads_pieces + [places],
            )[0][None]
            merge_pieces = over_reps(1)
            grad_merge = jnp.zeros((reps, head_run, features), F32)
            for k, piece in enumerate(merge_pieces):
                grad_merge = lax.dynamic_update_slice_in_dim(
                    grad_merge, piece.astype(F32)[None], rep ^ k, 0
                )
            grad_merge = grad_merge.reshape(1, depth, features)
        else:
            grad_heads = jnp.zeros((depth, 3, reps, width), F32)
            for k, piece in enumerate(heads_pieces):
                grad_heads = lax.dynamic_update_slice_in_dim(
                    grad_heads, piece.astype(F32).reshape(depth, 3, 1, width), rep ^ k, 2
                )
            grad_heads = grad_heads.reshape(1, depth, 3 * features)
            parts = owned(1)
            grad_merge = lax.psum(jnp.where(on_first, parts[0], parts[1]), "rep").astype(F32)[None]

        grad_up = jnp.zeros((depth, shards, reps, ff_own // shards), F32)
        for k, piece in enumerate(over_reps(2)):
            grad_up = lax.dynamic_update_slice_in_dim(
                grad_up, piece.astype(F32).reshape(depth, shards, 1, ff_own // shards), rep ^ k, 2
            )
        grad_up = grad_up.reshape(1, depth, ff)
        grad_down = jnp.zeros((reps, ff_own // shards, features), F32)
        for k, piece in enumerate(over_reps(3)):
            grad_down = lax.dynamic_update_slice_in_dim(
                grad_down, piece.astype(F32)[None], rep ^ k, 0
            )
        grad_down = grad_down.reshape(1, ff // shards, features)

    def by_section(pair):
        own = jnp.where(on_first, pair[0], pair[1])
        other = swap(jnp.where(on_first, pair[1], pair[0]))
        return jnp.concatenate(
            [jnp.where(on_first, own, other), jnp.where(on_first, other, own)], axis=0
        )[None]

    activations = by_section(outputs)
    input_grads = by_section(hidden_grads)
    (
        grad_first_gain,
        grad_first_shift,
        grad_query,
        grad_value,
        grad_output,
        grad_second_gain,
        grad_second_shift,
        grad_down_bias,
    ) = singles
    return (
        activations,
        input_grads,
        grad_heads,
        grad_merge,
        grad_up,
        grad_down,
        grad_first_gain,
        grad_first_shift,
        grad_query,
        grad_value,
        grad_output,
        grad_second_gain,
        grad_second_shift,
        grad_up_bias,
        grad_down_bias,
    )


def solution(mesh):
    rows = P(("shard", "rep"), None)
    matrix = P("section", "shard", None)
    line = P("section", "shard")
    return jax.shard_map(
        body,
        mesh=mesh,
        in_specs=(rows, rows) + (matrix,) * 4 + (line,) * 9 + (rows,),
        out_specs=(P("section", ("shard", "rep"), None),) * 2 + (matrix,) * 4 + (line,) * 9,
        check_vma=False,
    )
```
